32 devices in a mesh: seq: 4 (over y, core), shard: 8 (over z, x).
Axes of the slice: x: 2, y: 2, z: 4, core: 2. Of those that a mesh axis runs over, the one named last changes fastest.
Arguments:
- inputs: bfloat16 [8, 512, 2048], P('shard', 'seq'), may hold values from -6 to 6
- out_grad: bfloat16 [8, 512, 2048], P('shard', 'seq'), may hold values from -6 to 6
- segments: int32 [8, 512], P('shard', 'seq'), may hold values from 0 to 3, never falling along the last dimension, each value on 1 to 256 neighbouring positions
- w_in: float32 [2048, 24576], P(('seq', 'shard'))
- w_down: float32 [8192, 2048], P(('seq', 'shard'))
- conv_taps: float32 [2048, 3], P(('seq', 'shard'))
- norm_gains: float32 [2048, 2], P(('seq', 'shard'))
- m_in: float32 [2048, 24576], P(('seq', 'shard'))
- m_down: float32 [8192, 2048], P(('seq', 'shard'))
- m_taps: float32 [2048, 3], P(('seq', 'shard'))
- m_gains: float32 [2048, 2], P(('seq', 'shard'))
- v_in: float32 [2048, 24576], P(('seq', 'shard')), may hold values from 4.096 to 40.96
- v_down: float32 [8192, 2048], P(('seq', 'shard')), may hold values from 4.096 to 40.96
- v_taps: float32 [2048, 3], P(('seq', 'shard')), may hold values from 4.096 to 40.96
- v_gains: float32 [2048, 2], P(('seq', 'shard')), may hold values from 4.096 to 40.96
Outputs:
- block_out: bfloat16 [8, 512, 2048], P('shard', 'seq')
- input_grad: float32 [8, 512, 2048], P('shard', 'seq')
- grad_in: float32 [2048, 24576], P(('seq', 'shard'))
- grad_down: float32 [8192, 2048], P(('seq', 'shard'))
- grad_taps: float32 [2048, 3], P(('seq', 'shard'))
- grad_gains: float32 [2048, 2], P(('seq', 'shard'))
- new_m_in: float32 [2048, 24576], P(('seq', 'shard'))
- new_m_down: float32 [8192, 2048], P(('seq', 'shard'))
- new_m_taps: float32 [2048, 3], P(('seq', 'shard'))
- new_m_gains: float32 [2048, 2], P(('seq', 'shard'))
- new_v_in: float32 [2048, 24576], P(('seq', 'shard'))
- new_v_down: float32 [8192, 2048], P(('seq', 'shard'))
- new_v_taps: float32 [2048, 3], P(('seq', 'shard'))
- new_v_gains: float32 [2048, 2], P(('seq', 'shard'))
- new_w_in: float32 [2048, 24576], P(('seq', 'shard'))
- new_w_down: float32 [8192, 2048], P(('seq', 'shard'))
- new_w_taps: float32 [2048, 3], P(('seq', 'shard'))
- new_w_gains: float32 [2048, 2], P(('seq', 'shard'))
- lamb_norms: float32 [2, 8], replicated
The draws below stay inside these ranges and needn't reach their ends.
Inputs may be any that keep to these rules, and one draw needn't show every extreme that they name: `segments`: segment numbers never fall along a sequence; each of the 4 numbers holds 1 to 256 tokens of every sequence.
All inputs are finite; a program needn't handle non-finite values.
Results may differ from the reference program's by a relative error of at most 0.012.
The reference program's roundings to bfloat16 on the way count: a program that leaves them out, or rounds other values in their place, can miss the bound.
Values may be sent and summed in bfloat16 or wider, within the bound.
No kernel may reach another device: no remote copies, remote signals or barrier semaphores. Data moves between devices by JAX's collectives and lax.ppermute only.
A program may use at most 384 MiB of HBM per device.

```python
import math
import jax
import jax.numpy as jnp
import numpy as np
from jax import lax

D = 2048
FF = 8192
TAPS = 3
STEP = 4
SEQS = 8
LENGTH = 512
COLS = 24576
SEG_COUNT = 4
SEG_MOST = 256


def rising(key, rows, cols, scale):
    place = jnp.arange(rows, dtype=jnp.float32)[:, None] / rows
    base = jax.random.normal(key, (rows, cols), jnp.float32)
    return base * (0.5 + place) * scale


def moment_scale():
    return 0.1 * (SEQS * LENGTH) ** 0.5


def draw_w_in(key, part):
    return rising(jax.random.fold_in(key, 11), D, COLS, D ** (-0.5))


def draw_w_down(key, part):
    return rising(jax.random.fold_in(key, 12), FF, D, FF ** (-0.5))


def draw_conv_taps(key, part):
    return rising(jax.random.fold_in(key, 13), D, TAPS, 0.6)


def draw_norm_gains(key, part):
    place = jnp.arange(D, dtype=jnp.float32)[:, None] / D
    noise = jax.random.uniform(jax.random.fold_in(key, 14), (D, 2), jnp.float32, -1.0, 1.0)
    return (0.5 + place) * (1.0 + 0.3 * noise)


def draw_m_in(key, part):
    return rising(jax.random.fold_in(key, 21), D, COLS, moment_scale())


def draw_m_down(key, part):
    return rising(jax.random.fold_in(key, 22), FF, D, moment_scale())


def draw_m_taps(key, part):
    return rising(jax.random.fold_in(key, 23), D, TAPS, moment_scale())


def draw_m_gains(key, part):
    return rising(jax.random.fold_in(key, 24), D, 2, moment_scale())


def levels(rng, extent, cuts, smallest, top_value):
    def one(position, blocks):
        draws = jax.random.uniform(jax.random.fold_in(jax.random.fold_in(rng, 6), position), (blocks,), jnp.float32, smallest / len(cuts), top_value / len(cuts))
        return jnp.repeat(jnp.exp(draws), extent[position] // blocks).reshape((-1,) + (1,) * (len(extent) - position - 1))

    level = one(*cuts[0])
    for cut in cuts[1:]:
        level = level * one(*cut)
    return level


def length_profile(count, total, most, skew):
    weights = [(1 << 20) // math.isqrt(rank ** skew) + 1 for rank in range(2, count + 1)]
    surplus, given = total - most - (count - 1), [1] * (count - 1)
    while surplus > 0:
        candidates = [i for i in range(count - 1) if given[i] < most]
        pool, remaining = sum([weights[i] for i in candidates]), surplus
        for i in candidates:
            addition = min(most - given[i], max(1, remaining * weights[i] // pool), surplus)
            given[i] = given[i] + addition
            surplus = surplus - addition
    return np.array([most] + given)


def ragged(key, count, total, most, slope):
    if count == 2:
        one = jax.random.randint(key, (), max(1, total - most), min(most, total - 1) + 1)
        return jnp.stack([one, total - one])
    lengths = jnp.asarray(length_profile(count, total, most, slope), jnp.int32)
    couples = (count - 1) // 2
    giver, receiver = lengths[1:1 + 2 * couples:2], lengths[2:2 + 2 * couples:2]
    room = jnp.minimum(giver - 1, most - receiver)
    shifted = jax.random.randint(jax.random.fold_in(key, 1), (couples,), 0, 1 << 20) % (room + 1)
    lengths = lengths.at[1:1 + 2 * couples:2].set(giver - shifted).at[2:2 + 2 * couples:2].set(receiver + shifted)
    return lengths[jax.random.permutation(jax.random.fold_in(key, 2), count)]


def scatter_about(stream_key, dims, width, most, cuts=(), held_as=jnp.bfloat16):
    level = levels(stream_key, dims, cuts, -0.22, 0.18) if cuts else 1.0
    values = jax.random.normal(stream_key, dims, jnp.float32) * width * level
    return jnp.minimum(jnp.maximum(values, -most), most).astype(held_as)


def setup_inputs(seed: int = 0) -> dict:
    splits = jax.random.split(jax.random.key(seed), 16)
    return {
        "inputs": scatter_about(splits[0], (SEQS, LENGTH, D), 1.0, 6.0, ((0, 8), (1, 4))),
        "out_grad": scatter_about(splits[1], (SEQS, LENGTH, D), 1.0, 6.0, ((0, 8), (1, 4))),
        "segments": jax.vmap(lambda own: jnp.searchsorted(jnp.cumsum(ragged(own, SEG_COUNT, LENGTH, SEG_MOST, 2)), jnp.arange(LENGTH), side="right"))(jax.random.split(splits[2], SEQS)).reshape((SEQS, LENGTH)).astype(jnp.int32),
        "w_in": draw_w_in(jax.random.fold_in(splits[15], 71), 0),
        "w_down": draw_w_down(jax.random.fold_in(splits[15], 71), 0),
        "conv_taps": draw_conv_taps(jax.random.fold_in(splits[15], 71), 0),
        "norm_gains": draw_norm_gains(jax.random.fold_in(splits[15], 71), 0),
        "m_in": draw_m_in(jax.random.fold_in(splits[15], 71), 0),
        "m_down": draw_m_down(jax.random.fold_in(splits[15], 71), 0),
        "m_taps": draw_m_taps(jax.random.fold_in(splits[15], 71), 0),
        "m_gains": draw_m_gains(jax.random.fold_in(splits[15], 71), 0),
        "v_in": jnp.clip(jnp.exp(math.log(40.96) - 2.30258502 * jax.random.uniform(splits[11], (D, COLS), jnp.float32) ** levels(splits[11], (D, COLS), ((0, 32),), -0.2, 0.2)), 4.096, 40.96),
        "v_down": jnp.clip(jnp.exp(math.log(40.96) - 2.30258502 * jax.random.uniform(splits[12], (FF, D), jnp.float32) ** levels(splits[12], (FF, D), ((0, 32),), -0.2, 0.2)), 4.096, 40.96),
        "v_taps": jnp.clip(jnp.exp(math.log(40.96) - 2.30258502 * jax.random.uniform(splits[13], (D, TAPS), jnp.float32) ** levels(splits[13], (D, TAPS), ((0, 32),), -0.2, 0.2)), 4.096, 40.96),
        "v_gains": jnp.clip(jnp.exp(math.log(40.96) - 2.30258502 * jax.random.uniform(splits[14], (D, 2), jnp.float32) ** levels(splits[14], (D, 2), ((0, 32),), -0.2, 0.2)), 4.096, 40.96),
    }


EPS_NORM = 1e-05
BETA_ONE = 0.9
BETA_TWO = 0.999
EPS_ADAM = 1e-08
DECAY = 0.01
RATE = 0.3

@jax.custom_vjp
def low(v):
    return lax.optimization_barrier(v.astype(jnp.bfloat16)).astype(jnp.float32)

@jax.custom_vjp
def low_back(v):
    return v

def low_keep(v):
    return (low(v), None)

def low_pass(kept, grad):
    return (grad,)

def back_keep(v):
    return (v, None)

def back_low(kept, grad):
    return (low(grad),)
low.defvjp(low_keep, low_pass)
low_back.defvjp(back_keep, back_low)

def exact_dot(left, right):
    return jnp.dot(left, right, precision=lax.Precision.HIGHEST, preferred_element_type=jnp.float32)

def rms_norm(values, gain):
    scale = lax.rsqrt(lax.optimization_barrier(jnp.mean(values * values, axis=-1, keepdims=True)) + EPS_NORM)
    return values * scale * gain

def causal_conv(mixed_in, taps, seq_seg):
    total = taps[:, 0] * mixed_in
    for lag in range(1, TAPS):
        moved = jnp.concatenate([jnp.zeros((lag, mixed_in.shape[1]), mixed_in.dtype), mixed_in[:-lag]], 0)
        seg_moved = jnp.concatenate([jnp.full((lag,), -1, jnp.int32), seq_seg[:-lag].astype(jnp.int32)])
        keep = (seg_moved == seq_seg.astype(jnp.int32)).astype(mixed_in.dtype)
        total = total + taps[:, lag] * moved * keep[:, None]
    return total

def block(seq_x, seq_seg, w_in, w_down, taps, gains):
    norm_one = low(rms_norm(seq_x, gains[:, 0]))
    bcx = low_back(exact_dot(norm_one, w_in[:, :3 * D]))
    b_part = bcx[:, :D]
    c_part = bcx[:, D:2 * D]
    x_part = bcx[:, 2 * D:3 * D]
    mixed = low(c_part * causal_conv(b_part * x_part, taps, seq_seg))
    branch = low_back(exact_dot(mixed, w_in[:, 3 * D:4 * D]))
    middle = seq_x + branch
    norm_two = low(rms_norm(middle, gains[:, 1]))
    gate_up = low_back(exact_dot(norm_two, w_in[:, 4 * D:]))
    gate = gate_up[:, :FF]
    up_part = gate_up[:, FF:]
    hidden = low(jax.nn.silu(gate) * up_part)
    return middle + low_back(exact_dot(hidden, w_down))

def adam_direction(weight, grad, first, second):
    new_first = BETA_ONE * first + (1.0 - BETA_ONE) * grad
    new_second = BETA_TWO * second + (1.0 - BETA_TWO) * grad * grad
    first_hat = new_first / (1.0 - BETA_ONE ** STEP)
    second_hat = new_second / (1.0 - BETA_TWO ** STEP)
    direction = first_hat / (jnp.sqrt(second_hat) + EPS_ADAM) + DECAY * weight
    return (new_first, new_second, direction)

def piece_list(a_in, a_down, a_taps, a_gains):
    return [a_in[:, :3 * D], a_in[:, 3 * D:4 * D], a_in[:, 4 * D:4 * D + FF], a_in[:, 4 * D + FF:], a_down, a_taps, a_gains[:, 0], a_gains[:, 1]]

def reference(inputs, out_grad, segments, w_in, w_down, conv_taps, norm_gains, m_in, m_down, m_taps, m_gains, v_in, v_down, v_taps, v_gains):

    def whole(xs, a_in, a_down, a_taps, a_gains):
        used = (low(a_in), low(a_down), low(a_taps), low(a_gains))

        def one(item):
            return block(item[0], item[1], used[0], used[1], used[2], used[3])
        return lax.map(one, (xs, segments))
    outputs, pull = jax.vjp(whole, inputs.astype(jnp.float32), w_in, w_down, conv_taps, norm_gains)
    input_grad, grad_in, grad_down, grad_taps, grad_gains = pull(out_grad.astype(jnp.float32))
    new_m_in, new_v_in, dir_in = adam_direction(w_in, grad_in, m_in, v_in)
    new_m_down, new_v_down, dir_down = adam_direction(w_down, grad_down, m_down, v_down)
    new_m_taps, new_v_taps, dir_taps = adam_direction(conv_taps, grad_taps, m_taps, v_taps)
    new_m_gains, new_v_gains, dir_gains = adam_direction(norm_gains, grad_gains, m_gains, v_gains)
    weight_norm = jnp.sqrt(jnp.stack([jnp.sum(p * p) for p in piece_list(w_in, w_down, conv_taps, norm_gains)]))
    dir_norm = jnp.sqrt(jnp.stack([jnp.sum(p * p) for p in piece_list(dir_in, dir_down, dir_taps, dir_gains)]))
    ratio = -RATE * weight_norm / (dir_norm + 1e-06)
    ratio_cols = jnp.concatenate([jnp.full((3 * D,), ratio[0]), jnp.full((D,), ratio[1]), jnp.full((FF,), ratio[2]), jnp.full((FF,), ratio[3])])
    new_w_in = w_in + dir_in * ratio_cols[None, :]
    new_w_down = w_down + dir_down * ratio[4]
    new_w_taps = conv_taps + dir_taps * ratio[5]
    new_w_gains = norm_gains + dir_gains * jnp.stack([ratio[6], ratio[7]])[None, :]
    lamb_norms = jnp.stack([weight_norm, dir_norm])
    return (outputs.astype(jnp.bfloat16), input_grad, grad_in, grad_down, grad_taps, grad_gains, new_m_in, new_m_down, new_m_taps, new_m_gains, new_v_in, new_v_down, new_v_taps, new_v_gains, new_w_in, new_w_down, new_w_taps, new_w_gains, lamb_norms)
```

```python
import jax
import jax.numpy as jnp
from jax import lax
from jax.sharding import Mesh
from jax.sharding import PartitionSpec as P

D = 2048
FF = 8192
TAPS = 3
STEP = 4


EPS_NORM = 1e-05
BETA_ONE = 0.9
BETA_TWO = 0.999
EPS_ADAM = 1e-08
DECAY = 0.01
RATE = 0.3

AXES = ("y", "c", "zh", "zl", "x")
GROUP = ("c", "zl", "x")
TOKENS = ("zl", "x", "c")
LOW = jnp.bfloat16
WIDE = jnp.float32


def turned(value, axis, steps):
    n = lax.axis_size(axis)
    return lax.ppermute(value, axis, [(i, (i + steps) % n) for i in range(n)])


def moved(value, axis, steps):
    n = lax.axis_size(axis)
    return lax.ppermute(
        value, axis, [(i, i + steps) for i in range(max(0, -steps), min(n, n - steps))]
    )


def after(value, *others):
    return lax.optimization_barrier((value,) + others)[0]


def picked(value, index, dim):
    return lax.dynamic_index_in_dim(value, index, dim, keepdims=False)


def to_all(value):
    n = lax.axis_size(AXES)
    return lax.all_to_all(
        jnp.broadcast_to(value[None], (n,) + value.shape), AXES, 0, 0, tiled=True
    )


def reduced(value, axis, dim):
    n = lax.axis_size(axis)
    me = lax.axis_index(axis)
    own = picked(value, me, dim)
    for k in range(1, n):
        own = own + turned(
            picked(value, (me + k) % n, dim).astype(LOW), axis, k
        ).astype(WIDE)
    return own


def gather_tokens(value):
    return lax.all_gather(value, TOKENS, axis=0, tiled=True)


def scatter_tokens(partial):
    zl, x, c = (lax.axis_size(a) for a in TOKENS)
    blocks = partial.reshape(zl, x, c, -1, partial.shape[-1])
    own = reduced(blocks, "c", 2)
    half = own.shape[2] // 2
    first = reduced(reduced(own[:, :, :half], "zl", 0), "x", 0)
    second = reduced(reduced(own[:, :, half:], "x", 1), "zl", 0)
    return jnp.concatenate([first, second], 0)


def gather_rows(value):
    ny, nzh = lax.axis_size("y"), lax.axis_size("zh")
    yi, zi = lax.axis_index("y"), lax.axis_index("zh")
    out = jnp.zeros((ny, nzh) + value.shape, value.dtype)
    far = [(0, value)] + [(k, turned(value, "zh", k)) for k in range(1, nzh)]
    tail = (0,) * value.ndim
    for k, piece in far:
        for j in range(ny):
            got = turned(piece, "y", j) if j else piece
            place = ((yi - j) % ny, (zi - k) % nzh) + tail
            out = lax.dynamic_update_slice(out, got[None, None], place)
    return out, far[-1][1]


def scatter_rows(partial):
    ny, nzh = lax.axis_size("y"), lax.axis_size("zh")
    blocks = partial.reshape(ny, nzh, -1, partial.shape[-1])
    return reduced(reduced(blocks, "y", 0), "zh", 0)


def in_group(value):
    return lax.all_to_all(value, GROUP, 0, 0, tiled=True)


def norm_forward(values, gain):
    scale = lax.rsqrt(jnp.mean(values * values, axis=-1, keepdims=True) + EPS_NORM)
    return (values * scale * gain, scale)


def norm_backward(values, scale, gain, grad):
    along = grad * gain
    inner = jnp.mean(along * values, axis=-1, keepdims=True)
    d_values = scale * along - scale * scale * scale * values * inner
    d_gain = jnp.sum(grad * values * scale, axis=0)
    return (d_values, d_gain)


def times(left, right):
    return jnp.dot(left, right, preferred_element_type=WIDE)


def times_wide(left, right):
    return lax.dot_general(
        left, right, (((1,), (1,)), ((), ())), preferred_element_type=WIDE
    )


def over_tokens(left, right):
    return lax.dot_general(
        left, right, (((0,), (0,)), ((), ())), preferred_element_type=WIDE
    )


def piece_squares(a_in, a_down, a_taps, a_gains):
    parts = [
        a_in[:, : 3 * D],
        a_in[:, 3 * D : 4 * D],
        a_in[:, 4 * D : 4 * D + FF],
        a_in[:, 4 * D + FF :],
        a_down,
        a_taps,
        a_gains[:, 0],
        a_gains[:, 1],
    ]
    return jnp.stack([jnp.sum(p * p) for p in parts])


def adam_direction(weight, grad, first, second):
    new_first = BETA_ONE * first + (1.0 - BETA_ONE) * grad
    new_second = BETA_TWO * second + (1.0 - BETA_TWO) * grad * grad
    first_hat = new_first / (1.0 - BETA_ONE**STEP)
    second_hat = new_second / (1.0 - BETA_TWO**STEP)
    direction = first_hat / (jnp.sqrt(second_hat) + EPS_ADAM) + DECAY * weight
    return (new_first, new_second, direction)


def local(
    inputs,
    out_grad,
    segments,
    w_in,
    w_down,
    conv_taps,
    norm_gains,
    m_in,
    m_down,
    m_taps,
    m_gains,
    v_in,
    v_down,
    v_taps,
    v_gains,
):
    ny, nc, nzh, nzl, nx = (lax.axis_size(a) for a in AXES)
    yi, ci, zhi, zli, xi = (lax.axis_index(a) for a in AXES)
    members = nc * nzl * nx
    copies = ny * nzh
    own = inputs.shape[0] * inputs.shape[1]
    rows = w_in.shape[0]
    wide_rows = w_down.shape[0]
    channels = copies * rows
    hidden_own = copies * wide_rows
    seqs = nzl * nx
    span = nc * own

    def spread(a):
        lead = a.shape[0]
        return a.reshape(lead, ny, nc, nzh, -1).swapaxes(2, 3).reshape(lead, D)

    def unspread(a):
        lead = a.shape[0]
        return a.reshape(lead, ny, nzh, nc, -1).swapaxes(2, 3).reshape(lead, D)

    note = jnp.concatenate(
        [norm_gains.reshape(-1), conv_taps.reshape(-1), segments.reshape(-1).astype(WIDE)]
    )
    notes = to_all(note).reshape(ny, nc, nzh, nzl, nx, -1)
    gains = notes[..., : 2 * rows].reshape(D, 2).astype(LOW).astype(WIDE)
    gain_one = gains[:, 0]
    gain_two = gains[:, 1]
    of_group = picked(picked(picked(notes, xi, 4), zli, 3), ci, 1)
    taps = of_group[..., 2 * rows : 5 * rows].reshape(channels, TAPS).astype(LOW).astype(WIDE)
    ids_all = picked(notes[..., 5 * rows :], zhi, 2)
    ids = picked(ids_all, yi, 0).transpose(1, 2, 0, 3).reshape(seqs, span)
    prev_ids = picked(ids_all, jnp.maximum(yi - 1, 0), 0)[nc - 1, :, :, own - 2 :].reshape(seqs, 2)

    low_in = w_in.astype(LOW)
    low_down = w_down.astype(LOW)

    def by_member(part, kinds, width):
        split = part.reshape(rows, kinds, ny, nc, nzh, nzl, nx, width)
        return split.transpose(3, 5, 6, 0, 1, 2, 4, 7).reshape(members, rows, -1)

    def from_member(got, kinds, width):
        split = got.reshape(nc, nzl, nx, rows, kinds, ny, nzh, width)
        return split.transpose(3, 4, 5, 0, 6, 1, 2, 7).reshape(rows, -1)

    cols_p = in_group(by_member(low_in[:, : 3 * D], 3, rows))
    cols_gate = in_group(by_member(low_in[:, 4 * D : 4 * D + FF], 1, wide_rows))
    cols_up = in_group(by_member(low_in[:, 4 * D + FF :], 1, wide_rows))
    full_p, last = gather_rows(cols_p)
    full_p = full_p.reshape(D, 3 * channels)
    full_o, last = gather_rows(after(low_in[:, 3 * D : 4 * D], last))
    full_o = full_o.reshape(channels, D)
    full_gate, last = gather_rows(after(cols_gate, last))
    full_gate = full_gate.reshape(D, hidden_own)
    full_up, last = gather_rows(after(cols_up, last))
    full_up = full_up.reshape(D, hidden_own)
    full_down, last = gather_rows(after(low_down, last))
    full_down = full_down.reshape(hidden_own, D)

    values = inputs.reshape(own, D).astype(WIDE)
    norm_one, scale_one = norm_forward(values, gain_one)
    h_one = gather_tokens(spread(norm_one.astype(LOW)))
    grad_low = out_grad.reshape(own, D)
    grad_top = grad_low.astype(WIDE)
    d_ffn = gather_tokens(after(grad_low, h_one))
    bcx = times(h_one, full_p).reshape(seqs, span, 3, channels)
    b_part = bcx[:, :, 0]
    c_part = bcx[:, :, 1]
    x_part = bcx[:, :, 2]
    mixed_in = b_part * x_part
    prev_rows = moved(mixed_in[:, -2:], "y", 1)
    extended = jnp.concatenate([prev_rows, mixed_in], 1)
    ext_ids = jnp.concatenate([prev_ids, ids], 1)
    keeps = []
    conv = jnp.zeros((seqs, span, channels), WIDE)
    for lag in range(TAPS):
        keep = (ext_ids[:, 2 - lag : 2 - lag + span] == ids).astype(WIDE)[:, :, None]
        keeps.append(keep)
        conv = conv + taps[:, lag] * extended[:, 2 - lag : 2 - lag + span] * keep
    y_mix = (c_part * conv).astype(LOW).reshape(seqs * span, channels)
    middle = values + scatter_tokens(times(y_mix, full_o))

    norm_two, scale_two = norm_forward(middle, gain_two)
    h_two = gather_tokens(spread(norm_two.astype(LOW)))
    gate = times(h_two, full_gate)
    up_part = times(h_two, full_up)
    sig = jax.nn.sigmoid(gate)
    activated = gate * sig
    hidden = (activated * up_part).astype(LOW)
    d_hidden = times_wide(d_ffn, full_down)
    d_gate = (d_hidden * up_part * sig * (1.0 + gate * (1.0 - sig))).astype(LOW)
    d_up = (d_hidden * activated).astype(LOW)
    d_h_two = unspread(scatter_tokens(times_wide(d_gate, full_gate) + times_wide(d_up, full_up)))
    d_middle, d_gain_two = norm_backward(middle, scale_two, gain_two, d_h_two)
    d_middle = d_middle + grad_top

    d_branch = gather_tokens(d_middle.astype(LOW))
    d_mix = times_wide(d_branch, full_o).reshape(seqs, span, channels)
    d_c = d_mix * conv
    d_conv = d_mix * c_part
    d_extended = jnp.zeros((seqs, span + 2, channels), WIDE)
    tap_grads = []
    for lag in range(TAPS):
        counted = d_conv * keeps[lag]
        tap_grads.append(jnp.sum(counted * extended[:, 2 - lag : 2 - lag + span], axis=(0, 1)))
        d_extended = d_extended + jnp.pad(taps[:, lag] * counted, ((0, 0), (2 - lag, lag), (0, 0)))
    back_state = moved(d_extended[:, :2], "y", -1)
    d_mixed_in = d_extended[:, 2:] + jnp.pad(back_state, ((0, 0), (span - 2, 0), (0, 0)))
    d_bcx = jnp.stack([d_mixed_in * x_part, d_c, d_mixed_in * b_part], 2)
    d_bcx = d_bcx.astype(LOW).reshape(seqs * span, 3 * channels)
    d_h_one = unspread(scatter_tokens(times_wide(d_bcx, full_p)))
    d_values, d_gain_one = norm_backward(values, scale_one, gain_one, d_h_one)
    input_grad = (d_values + d_middle).reshape(inputs.shape)
    result = middle + scatter_tokens(times(hidden, full_down))
    block_out = result.astype(LOW).reshape(inputs.shape)

    def owned(partial, kinds, width):
        mine = scatter_rows(partial).astype(LOW)
        return from_member(in_group(mine.reshape(members, rows, -1)), kinds, width)

    grad_down = scatter_rows(over_tokens(hidden, d_ffn))
    grad_gate = owned(over_tokens(h_two, d_gate), 1, wide_rows)
    grad_up = owned(over_tokens(h_two, d_up), 1, wide_rows)
    grad_o = scatter_rows(over_tokens(y_mix, d_branch))
    grad_p = owned(over_tokens(h_one, d_bcx), 3, rows)
    grad_in = jnp.concatenate(
        [grad_p.astype(WIDE), grad_o, grad_gate.astype(WIDE), grad_up.astype(WIDE)], 1
    )
    gain_terms = jnp.stack([d_gain_one, d_gain_two], 1).reshape(-1, rows, 2)
    grad_gains = jnp.sum(lax.all_to_all(gain_terms, AXES, 0, 0, tiled=True), axis=0)
    tap_terms = jnp.stack(tap_grads, 1).reshape(copies, rows, TAPS)
    grad_taps = jnp.sum(lax.all_to_all(tap_terms, ("y", "zh"), 0, 0, tiled=True), axis=0)

    new_m_in, new_v_in, dir_in = adam_direction(w_in, grad_in, m_in, v_in)
    new_m_down, new_v_down, dir_down = adam_direction(w_down, grad_down, m_down, v_down)
    new_m_taps, new_v_taps, dir_taps = adam_direction(conv_taps, grad_taps, m_taps, v_taps)
    new_m_gains, new_v_gains, dir_gains = adam_direction(norm_gains, grad_gains, m_gains, v_gains)
    squares = jnp.stack(
        [
            piece_squares(w_in, w_down, conv_taps, norm_gains),
            piece_squares(dir_in, dir_down, dir_taps, dir_gains),
        ]
    )
    lamb_norms = jnp.sqrt(jnp.sum(to_all(squares), axis=0))
    ratio = -RATE * lamb_norms[0] / (lamb_norms[1] + 1e-06)
    ratio_cols = jnp.concatenate(
        [
            jnp.full((3 * D,), ratio[0]),
            jnp.full((D,), ratio[1]),
            jnp.full((FF,), ratio[2]),
            jnp.full((FF,), ratio[3]),
        ]
    )
    new_w_in = w_in + dir_in * ratio_cols[None, :]
    new_w_down = w_down + dir_down * ratio[4]
    new_w_taps = conv_taps + dir_taps * ratio[5]
    new_w_gains = norm_gains + dir_gains * jnp.stack([ratio[6], ratio[7]])[None, :]
    return (
        block_out,
        input_grad,
        grad_in,
        grad_down,
        grad_taps,
        grad_gains,
        new_m_in,
        new_m_down,
        new_m_taps,
        new_m_gains,
        new_v_in,
        new_v_down,
        new_v_taps,
        new_v_gains,
        new_w_in,
        new_w_down,
        new_w_taps,
        new_w_gains,
        lamb_norms,
    )


def solution(mesh):
    seq, shard = mesh.shape["seq"], mesh.shape["shard"]
    grid = Mesh(mesh.devices.reshape(seq // 2, 2, 2, 2, shard // 4), AXES)
    tokens = P(("zh", "zl", "x"), ("y", "c"), None)
    weights = P(AXES, None)
    return jax.shard_map(
        local,
        mesh=grid,
        in_specs=(tokens, tokens, P(("zh", "zl", "x"), ("y", "c"))) + (weights,) * 12,
        out_specs=(tokens, tokens) + (weights,) * 16 + (P(),),
        check_vma=False,
    )
```

```python
import functools

import jax
import jax.numpy as jnp
import numpy as np
from jax import lax
from jax.experimental import pallas as pl
from jax.experimental.pallas import tpu as pltpu
from jax.sharding import Mesh
from jax.sharding import PartitionSpec as P

D = 2048
FF = 8192
TAPS = 3
STEP = 4


EPS_NORM = 1e-05
BETA_ONE = 0.9
BETA_TWO = 0.999
EPS_ADAM = 1e-08
DECAY = 0.01
RATE = 0.3

AXES = ("y", "c", "h", "l")
FEED = ("h", "c")
FEED_COPIES = ("y", "l")
CONV = ("y", "c", "l")
LINES = ("l", "y")
LOW = jnp.bfloat16
WIDE = jnp.float32
ROOM = 56 * 1024 * 1024
SHORT = pl.CostEstimate(flops=1024, bytes_accessed=1024, transcendentals=0)


def turned(value, axes, steps):
    n = lax.axis_size(axes)
    names = (axes,) if isinstance(axes, str) else axes
    ordered = tuple(a for a in AXES if a in names)
    where = np.arange(n).reshape([lax.axis_size(a) for a in ordered])
    where = where.transpose([ordered.index(a) for a in names]).reshape(-1)
    pairs = [(int(where[i]), int(where[(i + steps) % n])) for i in range(n)]
    return lax.ppermute(value, ordered if len(names) > 1 else axes, pairs)


def tied(*values):
    return lax.optimization_barrier(values)


def picked(value, index, dim):
    return lax.dynamic_index_in_dim(value, index, dim, keepdims=False)


def exchanged(value, axes):
    return lax.all_to_all(value, axes, 0, 0, tiled=True)


def spread_to(value, axes):
    return exchanged(jnp.broadcast_to(value[None], (lax.axis_size(axes),) + value.shape), axes)


def rolled(value, axis, dim, sign):
    n, me = lax.axis_size(axis), lax.axis_index(axis)
    twice = jnp.concatenate([value, value], dim)
    return lax.dynamic_slice_in_dim(twice, (sign * me) % n, n, dim)


def placed(pieces, axis):
    n, me = len(pieces), lax.axis_index(axis)
    out = jnp.zeros((n,) + pieces[0].shape, pieces[0].dtype)
    for k, piece in enumerate(pieces):
        out = lax.dynamic_update_slice(
            out, piece[None], ((me + k) % n,) + (0,) * piece.ndim
        )
    return out


def norm_forward(values, gain):
    scale = lax.rsqrt(jnp.mean(values * values, axis=-1, keepdims=True) + EPS_NORM)
    return (values * scale * gain, scale)


def norm_backward(values, scale, gain, grad):
    along = grad * gain
    inner = jnp.mean(along * values, axis=-1, keepdims=True)
    d_values = scale * along - scale * scale * scale * values * inner
    d_gain = jnp.sum(grad * values * scale, axis=0)
    return (d_values, d_gain)


def times(left, right):
    return jnp.dot(left, right, preferred_element_type=WIDE)


def times_wide(left, right):
    return lax.dot_general(
        left, right, (((1,), (1,)), ((), ())), preferred_element_type=WIDE
    )


def over_tokens(left, right):
    return lax.dot_general(
        left, right, (((0,), (0,)), ((), ())), preferred_element_type=WIDE
    )


def adam_direction(weight, grad, first, second):
    new_first = BETA_ONE * first + (1.0 - BETA_ONE) * grad
    new_second = BETA_TWO * second + (1.0 - BETA_TWO) * grad * grad
    first_hat = new_first / (1.0 - BETA_ONE**STEP)
    second_hat = new_second / (1.0 - BETA_TWO**STEP)
    direction = first_hat / (jnp.sqrt(second_hat) + EPS_ADAM) + DECAY * weight
    return (new_first, new_second, direction)


def feed_kernel(h_ref, e_ref, g_ref, u_ref, d_ref, hid_ref, dg_ref, du_ref):
    step = 256
    for j in range(h_ref.shape[0] // step):
        at = slice(j * step, (j + 1) * step)
        gate = times(h_ref[at, :], g_ref[...])
        up = times(h_ref[at, :], u_ref[...])
        d_hidden = times_wide(e_ref[at, :], d_ref[...])
        sig = jax.nn.sigmoid(gate)
        activated = gate * sig
        hid_ref[at, :] = (activated * up).astype(LOW)
        dg_ref[at, :] = (d_hidden * up * (sig * (1.0 + gate * (1.0 - sig)))).astype(LOW)
        du_ref[at, :] = (d_hidden * activated).astype(LOW)


def feed(h, e, gate, up, down):
    count, features = h.shape[0], down.shape[0]
    tile = 256
    whole = pl.BlockSpec((count, D), lambda i: (0, 0), pipeline_mode=pl.Buffered(1))
    made = pl.BlockSpec((count, tile), lambda i: (0, i))
    return pl.pallas_call(
        feed_kernel,
        grid=(features // tile,),
        in_specs=[
            whole,
            whole,
            pl.BlockSpec((D, tile), lambda i: (0, i)),
            pl.BlockSpec((D, tile), lambda i: (0, i)),
            pl.BlockSpec((tile, D), lambda i: (i, 0)),
        ],
        out_specs=[made] * 3,
        out_shape=[jax.ShapeDtypeStruct((count, features), LOW)] * 3,
        compiler_params=pltpu.CompilerParams(vmem_limit_bytes=ROOM),
        cost_estimate=SHORT,
    )(h, e, gate, up, down)


def back_kernel(pairs, *refs):
    out_ref = refs[-1]
    total = None
    for left, right in zip(refs[:pairs], refs[pairs:-1]):
        part = times_wide(left[...], right[...])
        total = part if total is None else total + part
    out_ref[...] = total.astype(out_ref.dtype)


def back(lefts, right, dtype):
    count, width = lefts[0].shape
    tile = 512
    return pl.pallas_call(
        functools.partial(back_kernel, len(lefts)),
        grid=(D // tile,),
        in_specs=[
            pl.BlockSpec(a.shape, lambda i: (0, 0), pipeline_mode=pl.Buffered(1)) for a in lefts
        ]
        + [pl.BlockSpec((tile, width), lambda i, k=k: (i, k)) for k in range(len(lefts))],
        out_specs=pl.BlockSpec((count, tile), lambda i: (0, i)),
        out_shape=jax.ShapeDtypeStruct((count, D), dtype),
        compiler_params=pltpu.CompilerParams(vmem_limit_bytes=ROOM),
        cost_estimate=SHORT,
    )(*lefts, *[right] * len(lefts))


def both_kernel(count, wide, c_ref, *refs):
    out_ref = refs[-1]
    mine, other, rights = refs[:count], refs[count : 2 * count], refs[2 * count : -1]
    product = times_wide if wide else times

    def write(lefts):
        total = None
        for left, right in zip(lefts, rights):
            part = product(left[...], right[...])
            total = part if total is None else total + part
        out_ref[...] = total.astype(out_ref.dtype).reshape(out_ref.shape)

    @pl.when(pl.program_id(0) == 0)
    def _():
        write(mine)

    @pl.when(pl.program_id(0) == 1)
    def _():
        write(other)


def both_cores(core, mine, other, rights, own, wide):
    count, width = mine[0].shape
    tile = 512
    if wide:
        blocks = [pl.BlockSpec((tile, width), lambda g, i, c: (i, 0)) for _ in rights]
    else:
        blocks = [pl.BlockSpec((width, tile), lambda g, i, c: (0, i)) for _ in rights]
    return pl.pallas_call(
        functools.partial(both_kernel, len(mine), wide),
        grid_spec=pltpu.PrefetchScalarGridSpec(
            num_scalar_prefetch=1,
            grid=(2, D // tile),
            in_specs=[
                pl.BlockSpec(a.shape, lambda g, i, c: (0, 0), pipeline_mode=pl.Buffered(1))
                for a in mine + other
            ]
            + blocks,
            out_specs=pl.BlockSpec(
                (count // own, 1, own, tile), lambda g, i, c: (0, (c[0] + g) % 2, 0, i)
            ),
        ),
        out_shape=jax.ShapeDtypeStruct((count // own, 2, own, D), LOW),
        compiler_params=pltpu.CompilerParams(vmem_limit_bytes=ROOM),
        cost_estimate=SHORT,
    )(core, *mine, *other, *rights)


def weight_kernel(parts, outs, *refs):
    lefts, rights, out_ref = refs[:parts], refs[parts:-1], refs[-1]
    width = out_ref.shape[1] // outs
    for j in range(outs):
        total = None
        for i, left in enumerate(lefts):
            part = over_tokens(left[...], rights[i * outs + j][...])
            total = part if total is None else total + part
        out_ref[:, j * width : (j + 1) * width] = total.astype(out_ref.dtype)


def weight_grads(lefts, rights):
    parts, outs = len(lefts), len(rights[0])
    flat = [r for row in rights for r in row]
    rows, tile = lefts[0].shape[1], 512
    width = sum(r.shape[1] for r in rights[0])
    return pl.pallas_call(
        functools.partial(weight_kernel, parts, outs),
        grid=(rows // tile,),
        in_specs=[pl.BlockSpec((a.shape[0], tile), lambda i: (0, i)) for a in lefts]
        + [pl.BlockSpec(r.shape, lambda i: (0, 0), pipeline_mode=pl.Buffered(1)) for r in flat],
        out_specs=pl.BlockSpec((tile, width), lambda i: (i, 0)),
        out_shape=jax.ShapeDtypeStruct((rows, width), LOW),
        compiler_params=pltpu.CompilerParams(vmem_limit_bytes=ROOM),
        cost_estimate=SHORT,
    )(*lefts, *flat)


def prep_feed_kernel(nc, nh, w_ref, out_ref):
    width = out_ref.shape[2]
    for c in range(nc):
        for h in range(nh):
            at = (c * nh + h) * width
            out_ref[h * nc + c] = w_ref[:, at : at + width].astype(LOW)


def prep_feed(sizes, w, first):
    ny, nc, nh, _ = sizes
    rows, block = w.shape[0], FF // ny
    return pl.pallas_call(
        functools.partial(prep_feed_kernel, nc, nh),
        grid=(ny,),
        in_specs=[pl.BlockSpec((rows, block), lambda i: (0, first // block + i))],
        out_specs=pl.BlockSpec((nh * nc, rows, block // (nh * nc)), lambda i: (0, 0, i)),
        out_shape=jax.ShapeDtypeStruct((nh * nc, rows, FF // (nh * nc)), LOW),
        compiler_params=pltpu.CompilerParams(vmem_limit_bytes=ROOM),
        cost_estimate=SHORT,
    )(w)


def prep_conv_kernel(sizes, w_ref, out_ref):
    ny, nc, nh, nl = sizes
    rows = w_ref.shape[0]
    for yc in range(ny * nc):
        for k in range(nl):
            parts = [
                w_ref[:, ((yc * nh + h) * nl + k) * rows : ((yc * nh + h) * nl + k + 1) * rows]
                for h in range(nh)
            ]
            out_ref[yc * nl + k, 0] = jnp.concatenate(parts, 1).astype(LOW)


def prep_conv(sizes, w):
    ny, nc, nh, nl = sizes
    rows = w.shape[0]
    shape = (ny * nc * nl, 3, rows, nh * rows)
    return pl.pallas_call(
        functools.partial(prep_conv_kernel, sizes),
        grid=(3,),
        in_specs=[pl.BlockSpec((rows, D), lambda i: (0, i))],
        out_specs=pl.BlockSpec((shape[0], 1) + shape[2:], lambda i: (0, i, 0, 0)),
        out_shape=jax.ShapeDtypeStruct(shape, LOW),
        compiler_params=pltpu.CompilerParams(vmem_limit_bytes=ROOM),
        cost_estimate=SHORT,
    )(w)


def fold(values):
    rows, cols = values.shape
    total = values[:, :128]
    for k in range(1, cols // 128):
        total = total + values[:, 128 * k : 128 * (k + 1)]
    out = total[:8]
    for k in range(1, rows // 8):
        out = out + total[8 * k : 8 * (k + 1)]
    return out


def adam_step(first, grad, w_ref, m_ref, v_ref, grad_ref, nm_ref, nv_ref, dir_ref, sum_ref):
    weight = w_ref[...]
    new_m, new_v, direction = adam_direction(weight, grad, m_ref[...], v_ref[...])
    grad_ref[...] = grad
    nm_ref[...] = new_m
    nv_ref[...] = new_v
    dir_ref[...] = direction

    @pl.when(first)
    def _():
        sum_ref[...] = jnp.zeros_like(sum_ref)

    sum_ref[0, 0] += fold(weight * weight)
    sum_ref[0, 1] += fold(direction * direction)


def adam_gate_kernel(w_ref, m_ref, v_ref, got_ref, *refs):
    grad = jnp.concatenate([got_ref[h, 0] for h in range(got_ref.shape[0])], 1).astype(WIDE)
    adam_step(pl.program_id(0) == 0, grad, w_ref, m_ref, v_ref, *refs[-5:])


def adam_gate(sizes, w, m, v, got, kind, done=()):
    ny, nc, nh, _ = sizes
    rows = w.shape[0]
    part = got.shape[2] // (2 * ny)
    width = nh * part
    first = 4 * D + kind * FF
    column = pl.BlockSpec((rows, width), lambda b: (0, first // width + b))
    like = jax.ShapeDtypeStruct(w.shape, WIDE)
    return pl.pallas_call(
        adam_gate_kernel,
        grid=(ny * nc,),
        in_specs=[column] * 3
        + [pl.BlockSpec((nh, 1, rows, part), lambda b: (0, b % nc, 0, kind * ny + b // nc))]
        + [pl.BlockSpec(memory_space=pl.ANY) for _ in done],
        out_specs=[column] * 4 + [pl.BlockSpec((1, 2, 8, 128), lambda b: (0, 0, 0, 0))],
        out_shape=[like] * 4 + [jax.ShapeDtypeStruct((1, 2, 8, 128), WIDE)],
        input_output_aliases={4 + k: k for k in range(len(done))},
        compiler_params=pltpu.CompilerParams(vmem_limit_bytes=ROOM),
        cost_estimate=SHORT,
    )(w, m, v, got.reshape(nh, nc, rows, -1), *done)


def adam_plain_kernel(w_ref, m_ref, v_ref, g_ref, *refs):
    adam_step(pl.program_id(1) == 0, g_ref[...], w_ref, m_ref, v_ref, *refs[-5:])


def adam_columns(w, m, v, grad, first, kinds, done=()):
    rows = w.shape[0]
    width = 1024
    blocks = grad.shape[1] // (kinds * width)
    column = pl.BlockSpec((rows, width), lambda k, b: (0, first // width + k * blocks + b))
    like = jax.ShapeDtypeStruct(w.shape, WIDE)
    return pl.pallas_call(
        adam_plain_kernel,
        grid=(kinds, blocks),
        in_specs=[column] * 3
        + [pl.BlockSpec((rows, width), lambda k, b: (0, k * blocks + b))]
        + [pl.BlockSpec(memory_space=pl.ANY) for _ in done],
        out_specs=[column] * 4 + [pl.BlockSpec((1, 2, 8, 128), lambda k, b: (k, 0, 0, 0))],
        out_shape=[like] * 4 + [jax.ShapeDtypeStruct((kinds, 2, 8, 128), WIDE)],
        input_output_aliases={4 + k: k for k in range(len(done))},
        compiler_params=pltpu.CompilerParams(vmem_limit_bytes=ROOM),
        cost_estimate=SHORT,
    )(w, m, v, grad, *done)


def adam_down(w, m, v, grad):
    rows = 64
    block = pl.BlockSpec((rows, D), lambda k, i: (i, 0))
    like = jax.ShapeDtypeStruct(w.shape, WIDE)
    return pl.pallas_call(
        adam_plain_kernel,
        grid=(1, w.shape[0] // rows),
        in_specs=[block] * 4,
        out_specs=[block] * 4 + [pl.BlockSpec((1, 2, 8, 128), lambda k, i: (0, 0, 0, 0))],
        out_shape=[like] * 4 + [jax.ShapeDtypeStruct((1, 2, 8, 128), WIDE)],
        compiler_params=pltpu.CompilerParams(vmem_limit_bytes=ROOM),
        cost_estimate=SHORT,
    )(w, m, v, grad)


def adam_first_kernel(sizes, w_ref, m_ref, v_ref, got_ref, *refs):
    ny, nc, nh, nl = sizes
    rows = w_ref.shape[0]
    parts = []
    for yc in range(ny * nc):
        for h in range(nh):
            for k in range(nl):
                parts.append(got_ref[yc * nl + k, 0, :, h * rows : (h + 1) * rows])
    grad = jnp.concatenate(parts, 1).astype(WIDE)
    adam_step(pl.program_id(0) == 0, grad, w_ref, m_ref, v_ref, *refs[-5:])


def adam_first(sizes, w, m, v, got):
    rows = w.shape[0]
    column = pl.BlockSpec((rows, D), lambda i: (0, i))
    like = jax.ShapeDtypeStruct(w.shape, WIDE)
    return pl.pallas_call(
        functools.partial(adam_first_kernel, sizes),
        grid=(3,),
        in_specs=[column] * 3
        + [pl.BlockSpec((got.shape[0], 1) + got.shape[2:], lambda i: (0, i, 0, 0))],
        out_specs=[column] * 4 + [pl.BlockSpec((1, 2, 8, 128), lambda i: (0, 0, 0, 0))],
        out_shape=[like] * 4 + [jax.ShapeDtypeStruct((1, 2, 8, 128), WIDE)],
        compiler_params=pltpu.CompilerParams(vmem_limit_bytes=ROOM),
        cost_estimate=SHORT,
    )(w, m, v, got)


def step_kernel(ratio_ref, w_ref, dir_ref, *refs):
    refs[-1][...] = w_ref[...] + dir_ref[...] * ratio_ref[pl.program_id(0)]


def stepped(ratio, w, direction, first, kinds, blocks, width, done=None):
    rows = w.shape[0]
    column = pl.BlockSpec((rows, width), lambda k, b, r: (0, first + k * blocks + b))
    more = () if done is None else (done,)
    return pl.pallas_call(
        step_kernel,
        grid_spec=pltpu.PrefetchScalarGridSpec(
            num_scalar_prefetch=1,
            grid=(kinds, blocks),
            in_specs=[column] * 2 + [pl.BlockSpec(memory_space=pl.ANY) for _ in more],
            out_specs=column,
        ),
        out_shape=jax.ShapeDtypeStruct(w.shape, WIDE),
        input_output_aliases={3: 0} if more else {},
        compiler_params=pltpu.CompilerParams(vmem_limit_bytes=ROOM),
        cost_estimate=SHORT,
    )(ratio, w, direction, *more)


def local(
    inputs,
    out_grad,
    segments,
    w_in,
    w_down,
    conv_taps,
    norm_gains,
    m_in,
    m_down,
    m_taps,
    m_gains,
    v_in,
    v_down,
    v_taps,
    v_gains,
):
    sizes = tuple(lax.axis_size(a) for a in AXES)
    ny, nc, nh, nl = sizes
    yi, ci, hi, li = (lax.axis_index(a) for a in AXES)
    own = inputs.shape[0] * inputs.shape[1]
    rows = w_in.shape[0]
    wide_rows = w_down.shape[0]
    channels = nh * rows
    span = ny * nc * own
    conv_total = nl * span

    def feed_order(a):
        return a.reshape(own, ny, nc, nh, nl, rows).transpose(0, 1, 4, 3, 2, 5).reshape(own, D)

    def from_feed_order(a):
        return a.reshape(own, ny, nl, nh, nc, rows).transpose(0, 1, 4, 3, 2, 5).reshape(own, D)

    def conv_order(a):
        return rolled(a.reshape(own, ny * nc, nh, -1).swapaxes(1, 2), "h", 1, 1).reshape(own, D)

    def from_conv_order(a):
        return rolled(a.reshape(own, nh, ny * nc, -1), "h", 1, -1).swapaxes(1, 2).reshape(own, D)

    def near(value, axes, first=1, last=None):
        last = lax.axis_size(axes) if last is None else last
        return [turned(value, axes, -k) for k in range(first, last)]

    def ring(value, axis):
        pieces = [value]
        for _ in range(1, lax.axis_size(axis)):
            pieces.append(turned(pieces[-1], axis, -1))
        return pieces

    def ring_sum(blocks, axis):
        n = lax.axis_size(axis)
        passed = blocks[n - 1]
        for k in range(n - 2, -1, -1):
            passed = turned(passed.astype(LOW), axis, 1).astype(WIDE) + blocks[k].astype(WIDE)
        return passed

    def with_core(pieces):
        mine = jnp.concatenate(pieces, 0)
        return mine, turned(mine, "c", 1)

    def scatter(other, mine, axes):
        both = turned(other, "c", 1)
        both = (mine() + both.astype(WIDE)).reshape(-1, own, D)
        sent = [turned(both[k].astype(LOW), axes, k) for k in range(1, both.shape[0])]
        return both[0], sent

    def total(first, sent):
        for s in sent:
            first = first + s.astype(WIDE)
        return first

    def out_order(a):
        return rolled(a, "h", 0, -1)

    note = jnp.concatenate(
        [norm_gains.reshape(-1), conv_taps.reshape(-1), segments.reshape(-1).astype(WIDE)]
    )
    low_o = w_in[:, 3 * D : 4 * D].astype(LOW)
    notes, p_cols = tied(spread_to(note, AXES), prep_conv(sizes, w_in))
    o_pieces = [low_o] + near(low_o, "h")
    notes = notes.reshape(sizes + (-1,))
    gains = notes[..., : 2 * rows].reshape(D, 2).astype(LOW).astype(WIDE)
    gain_one = gains[:, 0]
    gain_two = gains[:, 1]
    of_group = picked(picked(picked(notes, li, 3), ci, 1), yi, 0)
    taps = of_group[:, 2 * rows : 5 * rows].reshape(channels, TAPS).astype(LOW).astype(WIDE)
    ids = picked(notes[..., 5 * rows :], hi, 2).transpose(2, 0, 1, 3).reshape(nl, span)

    def as_rows(a):
        return a.reshape(-1, a.shape[-1])

    grad_low = out_grad.reshape(own, D)
    grad_top = grad_low.astype(WIDE)
    e_all = lax.all_gather(grad_low, FEED, axis=0)
    down = lax.all_gather(w_down.astype(LOW), FEED_COPIES, axis=0, tiled=True)
    values = inputs.reshape(own, D).astype(WIDE)
    norm_one, scale_one = norm_forward(values, gain_one)
    low_one = conv_order(norm_one.astype(LOW))
    mine, other = with_core([low_one] + near(low_one, LINES))
    cols_p, gate_cols, *o_pieces = tied(
        exchanged(p_cols, CONV), prep_feed(sizes, w_in, 4 * D), *o_pieces
    )
    gate_cols, cols_p, mine, other = tied(exchanged(gate_cols, FEED), cols_p, mine, other)
    gate_w = lax.all_gather(as_rows(gate_cols), FEED_COPIES, axis=0, tiled=True)
    o_w = placed(o_pieces, "h").reshape(channels, D)
    pieces = ring(cols_p.swapaxes(1, 2).reshape(-1, 3 * channels), "h")
    pieces[-1], up_cols = tied(pieces[-1], prep_feed(sizes, w_in, 4 * D + FF))
    up_cols = exchanged(up_cols, FEED)
    p_w = jnp.concatenate(pieces, 0)

    h_one = jnp.zeros((ny * nl, nc, own, D), LOW)
    for k, part in enumerate((mine, other)):
        part = rolled(part.reshape(-1, 1, own, D), LINES, 0, -1)
        h_one = lax.dynamic_update_slice(h_one, part, (0, (ci + k) % nc, 0, 0))
    h_one = h_one.reshape(conv_total, D)
    bcx = times(h_one, p_w).reshape(nl, span, 3 * channels)
    b_part = bcx[:, :, :channels]
    c_part = bcx[:, :, channels : 2 * channels]
    x_part = bcx[:, :, 2 * channels :]
    mixed_in = b_part * x_part
    extended = jnp.pad(mixed_in, ((0, 0), (2, 0), (0, 0)))
    ext_ids = jnp.pad(ids, ((0, 0), (2, 0)), constant_values=-1.0)
    keeps = []
    conv = jnp.zeros((nl, span, channels), WIDE)
    for lag in range(TAPS):
        keep = (ext_ids[:, 2 - lag : 2 - lag + span] == ids).astype(WIDE)[:, :, None]
        keeps.append(keep)
        conv = conv + taps[:, lag] * extended[:, 2 - lag : 2 - lag + span] * keep
    y_mix = (c_part * conv).astype(LOW)

    def by_core(value):
        parts = rolled(value.reshape(ny * nl, nc, own, -1), LINES, 0, 1)
        return [picked(parts, (ci + k) % nc, 1).reshape(ny * nl * own, -1) for k in range(nc)]

    y_mine, y_other = by_core(y_mix)
    both, sent = scatter(times(y_other, o_w).astype(LOW), lambda: times(y_mine, o_w), LINES)
    both, up_cols = tied(both, up_cols)
    up_w = lax.all_gather(as_rows(up_cols), FEED_COPIES, axis=0, tiled=True)
    *sent, e_all = tied(*sent, e_all)
    middle = values + total(both, sent)
    e_all = e_all.reshape(nh, nc, own, D)
    e_mine, e_other = (picked(e_all, (ci + k) % nc, 1).reshape(-1, D) for k in range(nc))

    norm_two, scale_two = norm_forward(middle, gain_two)
    low_two = feed_order(norm_two.astype(LOW))
    h_mine = placed([low_two] + near(low_two, "h"), "h").reshape(-1, D)
    h_other = turned(h_mine, "c", 1)
    hid_mine, dg_mine, du_mine = feed(h_mine, e_mine, gate_w, up_w, down)
    hid_other, dg_other, du_other = feed(h_other, e_other, gate_w, up_w, down)
    core = ci.reshape(1).astype(jnp.int32)

    def summed(part, axes):
        return lax.psum_scatter(part, axes, scatter_dimension=0, tiled=True)

    d_h_two = both_cores(core, [dg_mine, du_mine], [dg_other, du_other], [gate_w, up_w], own, True)
    d_h_two, h_mine = tied(d_h_two, h_mine)
    d_h_two = summed(d_h_two.reshape(-1, D), FEED).astype(WIDE)
    part_feed = weight_grads([h_mine, h_other], [[dg_mine, du_mine], [dg_other, du_other]])
    part_feed, hid_mine = tied(part_feed, hid_mine)
    part_down = weight_grads([hid_mine, hid_other], [[e_mine], [e_other]])
    out_part = both_cores(core, [hid_mine], [hid_other], [down], own, False)
    d_h_two, part_down, part_feed, out_part = tied(d_h_two, part_down, part_feed, out_part)
    out_sum = summed(out_part.reshape(-1, D), FEED)
    d_middle, d_gain_two = norm_backward(middle, scale_two, gain_two, from_feed_order(d_h_two))
    d_middle = d_middle + grad_top

    low_branch = d_middle.astype(LOW)
    do_mine, do_other = with_core([low_branch] + near(low_branch, LINES))
    do_mine, do_other, part_feed = tied(do_mine, do_other, part_feed)
    got_feed = summed(part_feed, FEED_COPIES)
    part_o = over_tokens(y_mine, do_mine) + over_tokens(y_other, do_other)
    part_o = rolled(part_o.reshape(nh, rows, D), "h", 0, 1)
    sent_o = [turned(part_o[k].astype(LOW), "h", k) for k in range(1, nh)]
    d_mix = jnp.zeros((ny * nl, nc, own, channels), WIDE)
    for k, part in enumerate((do_mine, do_other)):
        part = rolled(times_wide(part, o_w).reshape(-1, 1, own, channels), LINES, 0, -1)
        d_mix = lax.dynamic_update_slice(d_mix, part, (0, (ci + k) % nc, 0, 0))
    d_mix = d_mix.reshape(nl, span, channels)
    d_c = d_mix * conv
    d_conv = d_mix * c_part
    d_extended = jnp.zeros((nl, span + 2, channels), WIDE)
    tap_grads = []
    for lag in range(TAPS):
        counted = d_conv * keeps[lag]
        tap_grads.append(jnp.sum(counted * extended[:, 2 - lag : 2 - lag + span], axis=(0, 1)))
        d_extended = d_extended + jnp.pad(taps[:, lag] * counted, ((0, 0), (2 - lag, lag), (0, 0)))
    d_mixed_in = d_extended[:, 2:]
    d_bcx = jnp.concatenate([d_mixed_in * x_part, d_c, d_mixed_in * b_part], 2).astype(LOW)

    part_p = weight_grads([h_one], [[d_bcx.reshape(conv_total, -1)]]).reshape(nh, -1, 3 * channels)
    part_p, d_bcx, part_down, out_sum, *sent_o = tied(part_p, d_bcx, part_down, out_sum, *sent_o)
    grad_o = total(part_o[0], sent_o)
    grad_down = summed(part_down, FEED_COPIES)
    part_p = ring_sum(list(part_p), "h").astype(LOW)
    db_mine, db_other = by_core(d_bcx)
    other = back([db_other], p_w, LOW)
    other, db_mine = tied(other, db_mine)
    both, sent = scatter(other, lambda: back([db_mine], p_w, WIDE), LINES)
    got_feed, part_p = tied(got_feed, part_p)
    got_feed, part_p, both = tied(exchanged(got_feed.reshape(nh * nc, rows, -1), FEED), part_p, both)
    got_p = exchanged(part_p.reshape(ny * nc * nl, rows, 3, channels).swapaxes(1, 2), CONV)
    d_h_one = total(both, sent)
    d_values, d_gain_one = norm_backward(values, scale_one, gain_one, from_conv_order(d_h_one))
    input_grad = (d_values + d_middle).reshape(inputs.shape)

    tap_terms = jnp.stack(tap_grads, 1).reshape(1, 1, nh, 1, rows, TAPS)
    tap_terms = lax.dynamic_update_slice(
        jnp.zeros(sizes + (rows, TAPS), WIDE), tap_terms, (yi, ci, 0, li, 0, 0)
    )
    gain_terms = jnp.stack([d_gain_one, d_gain_two], 1).reshape(sizes + (rows, 2))
    terms = jnp.concatenate([tap_terms, gain_terms], -1).reshape(-1, rows, TAPS + 2)
    got_p, terms = tied(got_p, terms)
    terms = exchanged(terms, AXES)
    *done, sums_p = adam_first(sizes, w_in, m_in, v_in, got_p)
    *done, sums_o = adam_columns(w_in, m_in, v_in, grad_o, 3 * D, 1, done)
    *done, sums_gate = adam_gate(sizes, w_in, m_in, v_in, got_feed, 0, done)
    *done, sums_up = adam_gate(sizes, w_in, m_in, v_in, got_feed, 1, done)
    grad_down, sums_up = tied(grad_down, sums_up)
    grad_down = grad_down.astype(WIDE)
    grad_down, new_m_down, new_v_down, dir_down, sums_down = adam_down(w_down, m_down, v_down, grad_down)
    grad_in, new_m_in, new_v_in, dir_in = done
    block_out = (middle + out_sum.astype(WIDE)).astype(LOW).reshape(inputs.shape)
    terms = jnp.sum(terms, axis=0)
    grad_taps, grad_gains = terms[:, :TAPS], terms[:, TAPS:]
    new_m_taps, new_v_taps, dir_taps = adam_direction(conv_taps, grad_taps, m_taps, v_taps)
    new_m_gains, new_v_gains, dir_gains = adam_direction(norm_gains, grad_gains, m_gains, v_gains)

    def lanes(a):
        return jnp.pad(jnp.sum(a * a, axis=0), (0, 128 - a.shape[1]))

    def small(taps_like, gains_like):
        return jnp.stack(
            [lanes(taps_like), lanes(gains_like[:, :1]), lanes(gains_like[:, 1:])], 0
        )

    sums = jnp.concatenate(
        [
            jnp.sum(jnp.concatenate([sums_p, sums_o, sums_gate, sums_up, sums_down], 0), axis=2),
            jnp.stack([small(conv_taps, norm_gains), small(dir_taps, dir_gains)], 1),
        ],
        0,
    )
    lamb_norms = jnp.sqrt(jnp.sum(spread_to(sums, AXES), axis=(0, 3)).T)
    ratio = -RATE * lamb_norms[0] / (lamb_norms[1] + 1e-06)
    width = 2048
    new_w_down = w_down + dir_down * ratio[4]
    new_w_in = stepped(ratio[:1], w_in, dir_in, 0, 1, 3 * D // width, width)
    new_w_in = stepped(ratio[1:2], w_in, dir_in, 3 * D // width, 1, D // width, width, new_w_in)
    new_w_in = stepped(ratio[2:4], w_in, dir_in, 4 * D // width, 2, FF // width, width, new_w_in)
    new_w_taps = conv_taps + dir_taps * ratio[5]
    new_w_gains = norm_gains + dir_gains * ratio[6:][None, :]
    return (
        block_out,
        input_grad,
        grad_in,
        grad_down,
        grad_taps,
        grad_gains,
        new_m_in,
        new_m_down,
        new_m_taps,
        new_m_gains,
        new_v_in,
        new_v_down,
        new_v_taps,
        new_v_gains,
        new_w_in,
        new_w_down,
        new_w_taps,
        new_w_gains,
        lamb_norms,
    )


def solution(mesh):
    seq, shard = mesh.shape["seq"], mesh.shape["shard"]
    grid = Mesh(mesh.devices.reshape(seq // 2, 2, 4, shard // 4), AXES)
    tokens = P(("h", "l"), ("y", "c"), None)
    weights = P(AXES, None)
    return jax.shard_map(
        local,
        mesh=grid,
        in_specs=(tokens, tokens, P(("h", "l"), ("y", "c"))) + (weights,) * 12,
        out_specs=(tokens, tokens) + (weights,) * 16 + (P(),),
        check_vma=False,
    )
```

```python
import functools

import jax
import jax.numpy as jnp
import numpy as np
from jax import lax
from jax.experimental import pallas as pl
from jax.experimental.pallas import tpu as pltpu
from jax.sharding import Mesh
from jax.sharding import PartitionSpec as P

D = 2048
FF = 8192
TAPS = 3
STEP = 4


EPS_NORM = 1e-05
BETA_ONE = 0.9
BETA_TWO = 0.999
EPS_ADAM = 1e-08
DECAY = 0.01
RATE = 0.3

AXES = ("y", "c", "h", "l")
FEED = ("h", "c")
FEED_COPIES = ("y", "l")
CONV = ("y", "c", "l")
LINES = ("l", "y")
LOW = jnp.bfloat16
WIDE = jnp.float32
ROOM = 56 * 1024 * 1024
SHORT = pl.CostEstimate(flops=1024, bytes_accessed=1024, transcendentals=0)


def turned(value, axes, steps):
    n = lax.axis_size(axes)
    names = (axes,) if isinstance(axes, str) else axes
    ordered = tuple(a for a in AXES if a in names)
    where = np.arange(n).reshape([lax.axis_size(a) for a in ordered])
    where = where.transpose([ordered.index(a) for a in names]).reshape(-1)
    pairs = [(int(where[i]), int(where[(i + steps) % n])) for i in range(n)]
    return lax.ppermute(value, ordered if len(names) > 1 else axes, pairs)


def tied(*values):
    return lax.optimization_barrier(values)


def picked(value, index, dim):
    return lax.dynamic_index_in_dim(value, index, dim, keepdims=False)


def exchanged(value, axes):
    return lax.all_to_all(value, axes, 0, 0, tiled=True)


def spread_to(value, axes):
    return exchanged(jnp.broadcast_to(value[None], (lax.axis_size(axes),) + value.shape), axes)


def rolled(value, axis, dim, sign):
    n, me = lax.axis_size(axis), lax.axis_index(axis)
    twice = jnp.concatenate([value, value], dim)
    return lax.dynamic_slice_in_dim(twice, (sign * me) % n, n, dim)


def placed(pieces, axis):
    n, me = len(pieces), lax.axis_index(axis)
    out = jnp.zeros((n,) + pieces[0].shape, pieces[0].dtype)
    for k, piece in enumerate(pieces):
        out = lax.dynamic_update_slice(
            out, piece[None], ((me + k) % n,) + (0,) * piece.ndim
        )
    return out


def norm_forward(values, gain):
    scale = lax.rsqrt(jnp.mean(values * values, axis=-1, keepdims=True) + EPS_NORM)
    return (values * scale * gain, scale)


def norm_backward(values, scale, gain, grad):
    along = grad * gain
    inner = jnp.mean(along * values, axis=-1, keepdims=True)
    d_values = scale * along - scale * scale * scale * values * inner
    d_gain = jnp.sum(grad * values * scale, axis=0)
    return (d_values, d_gain)


def times(left, right):
    return jnp.dot(left, right, preferred_element_type=WIDE)


def times_wide(left, right):
    return lax.dot_general(
        left, right, (((1,), (1,)), ((), ())), preferred_element_type=WIDE
    )


def over_tokens(left, right):
    return lax.dot_general(
        left, right, (((0,), (0,)), ((), ())), preferred_element_type=WIDE
    )


def adam_direction(weight, grad, first, second):
    new_first = BETA_ONE * first + (1.0 - BETA_ONE) * grad
    new_second = BETA_TWO * second + (1.0 - BETA_TWO) * grad * grad
    first_hat = new_first / (1.0 - BETA_ONE**STEP)
    second_hat = new_second / (1.0 - BETA_TWO**STEP)
    direction = first_hat / (jnp.sqrt(second_hat) + EPS_ADAM) + DECAY * weight
    return (new_first, new_second, direction)


def assembled_kernel(me_ref, *refs):
    out_ref, n = refs[-1], len(refs) - 1
    for k in range(n):
        out_ref[pl.ds((me_ref[0] + k) % n, 1)] = refs[k][...][None]


def assembled(me, pieces):
    rows, cols = pieces[0].shape
    n = len(pieces)
    out = pl.pallas_call(
        assembled_kernel,
        in_specs=[pl.BlockSpec(memory_space=pltpu.SMEM)]
        + [pl.BlockSpec(memory_space=pltpu.VMEM) for _ in pieces],
        out_specs=pl.BlockSpec(memory_space=pltpu.VMEM),
        out_shape=jax.ShapeDtypeStruct((n, rows, cols), LOW),
        compiler_params=pltpu.CompilerParams(vmem_limit_bytes=ROOM),
        cost_estimate=SHORT,
    )(me.reshape(1).astype(jnp.int32), *pieces)
    return out.reshape(n * rows, cols)


def interleaved_kernel(place_ref, mine_ref, other_ref, out_ref):
    out_ref[0, pl.ds(place_ref[1], 1)] = mine_ref[...][None]
    out_ref[0, pl.ds(1 - place_ref[1], 1)] = other_ref[...][None]


def interleaved(place, mine, other, own):
    n, cols = mine.shape[0] // own, mine.shape[1]
    block = pl.BlockSpec((own, cols), lambda i, p: (i, 0))
    return pl.pallas_call(
        interleaved_kernel,
        grid_spec=pltpu.PrefetchScalarGridSpec(
            num_scalar_prefetch=1,
            grid=(n,),
            in_specs=[block, block],
            out_specs=pl.BlockSpec((1, 2, own, cols), lambda i, p: ((p[0] + i) % n, 0, 0, 0)),
        ),
        out_shape=jax.ShapeDtypeStruct((n, 2, own, cols), mine.dtype),
        compiler_params=pltpu.CompilerParams(vmem_limit_bytes=ROOM),
        cost_estimate=SHORT,
    )(place.astype(jnp.int32), mine, other)


def feed_kernel(c_ref, h_ref, e_ref, g_ref, u_ref, d_ref, hid_ref, dg_ref, du_ref):
    step = 256
    grads = e_ref[...].reshape(h_ref.shape)
    for j in range(h_ref.shape[0] // step):
        at = slice(j * step, (j + 1) * step)
        gate = times(h_ref[at, :], g_ref[...])
        up = times(h_ref[at, :], u_ref[...])
        d_hidden = times_wide(grads[at, :], d_ref[...])
        sig = jax.nn.sigmoid(gate)
        activated = gate * sig
        hid_ref[at, :] = (activated * up).astype(LOW)
        dg_ref[at, :] = (d_hidden * up * (sig * (1.0 + gate * (1.0 - sig)))).astype(LOW)
        du_ref[at, :] = (d_hidden * activated).astype(LOW)


def feed(core, h, e, gate, up, down):
    count, features = h.shape[0], down.shape[0]
    tile = 256
    made = pl.BlockSpec((count, tile), lambda i, c: (0, i))
    return pl.pallas_call(
        feed_kernel,
        grid_spec=pltpu.PrefetchScalarGridSpec(
            num_scalar_prefetch=1,
            grid=(features // tile,),
            in_specs=[
                pl.BlockSpec((count, D), lambda i, c: (0, 0), pipeline_mode=pl.Buffered(1)),
                pl.BlockSpec(
                    (e.shape[0], 1) + e.shape[2:],
                    lambda i, c: (0, c[0], 0, 0),
                    pipeline_mode=pl.Buffered(1),
                ),
                pl.BlockSpec((D, tile), lambda i, c: (0, i)),
                pl.BlockSpec((D, tile), lambda i, c: (0, i)),
                pl.BlockSpec((tile, D), lambda i, c: (i, 0)),
            ],
            out_specs=[made] * 3,
        ),
        out_shape=[jax.ShapeDtypeStruct((count, features), LOW)] * 3,
        compiler_params=pltpu.CompilerParams(vmem_limit_bytes=ROOM),
        cost_estimate=SHORT,
    )(core, h, e, gate, up, down)


def down_kernel(c_ref, mine_ref, other_ref, mine_e_ref, other_e_ref, out_ref):
    rows = mine_ref.shape[0]
    total = over_tokens(mine_ref[...], mine_e_ref[...].reshape(rows, -1))
    total += over_tokens(other_ref[...], other_e_ref[...].reshape(rows, -1))
    out_ref[...] = total.astype(out_ref.dtype)


def down_grads(core, mine, other, e):
    count, features = mine.shape
    tile = 512
    side = (e.shape[0], 1) + e.shape[2:]
    return pl.pallas_call(
        down_kernel,
        grid_spec=pltpu.PrefetchScalarGridSpec(
            num_scalar_prefetch=1,
            grid=(features // tile,),
            in_specs=[
                pl.BlockSpec((count, tile), lambda i, c: (0, i)),
                pl.BlockSpec((count, tile), lambda i, c: (0, i)),
                pl.BlockSpec(side, lambda i, c: (0, c[0], 0, 0), pipeline_mode=pl.Buffered(1)),
                pl.BlockSpec(side, lambda i, c: (0, 1 - c[0], 0, 0), pipeline_mode=pl.Buffered(1)),
            ],
            out_specs=pl.BlockSpec((tile, D), lambda i, c: (i, 0)),
        ),
        out_shape=jax.ShapeDtypeStruct((features, D), LOW),
        compiler_params=pltpu.CompilerParams(vmem_limit_bytes=ROOM),
        cost_estimate=SHORT,
    )(core, mine, other, e, e)


def back_kernel(pairs, *refs):
    out_ref = refs[-1]
    total = None
    for left, right in zip(refs[:pairs], refs[pairs:-1]):
        part = times_wide(left[...], right[...])
        total = part if total is None else total + part
    out_ref[...] = total.astype(out_ref.dtype)


def back(lefts, right, dtype):
    count, width = lefts[0].shape
    tile = 512
    return pl.pallas_call(
        functools.partial(back_kernel, len(lefts)),
        grid=(D // tile,),
        in_specs=[
            pl.BlockSpec(a.shape, lambda i: (0, 0), pipeline_mode=pl.Buffered(1)) for a in lefts
        ]
        + [pl.BlockSpec((tile, width), lambda i, k=k: (i, k)) for k in range(len(lefts))],
        out_specs=pl.BlockSpec((count, tile), lambda i: (0, i)),
        out_shape=jax.ShapeDtypeStruct((count, D), dtype),
        compiler_params=pltpu.CompilerParams(vmem_limit_bytes=ROOM),
        cost_estimate=SHORT,
    )(*lefts, *[right] * len(lefts))


def both_kernel(count, wide, c_ref, *refs):
    out_ref = refs[-1]
    mine, other, rights = refs[:count], refs[count : 2 * count], refs[2 * count : -1]
    product = times_wide if wide else times

    def write(lefts):
        total = None
        for left, right in zip(lefts, rights):
            part = product(left[...], right[...])
            total = part if total is None else total + part
        out_ref[...] = total.astype(out_ref.dtype).reshape(out_ref.shape)

    @pl.when(pl.program_id(0) == 0)
    def _():
        write(mine)

    @pl.when(pl.program_id(0) == 1)
    def _():
        write(other)


def both_cores(core, mine, other, rights, own, wide):
    count, width = mine[0].shape
    tile = 512
    if wide:
        blocks = [pl.BlockSpec((tile, width), lambda g, i, c: (i, 0)) for _ in rights]
    else:
        blocks = [pl.BlockSpec((width, tile), lambda g, i, c: (0, i)) for _ in rights]
    return pl.pallas_call(
        functools.partial(both_kernel, len(mine), wide),
        grid_spec=pltpu.PrefetchScalarGridSpec(
            num_scalar_prefetch=1,
            grid=(2, D // tile),
            in_specs=[
                pl.BlockSpec(a.shape, lambda g, i, c: (0, 0), pipeline_mode=pl.Buffered(1))
                for a in mine + other
            ]
            + blocks,
            out_specs=pl.BlockSpec(
                (count // own, 1, own, tile), lambda g, i, c: (0, (c[0] + g) % 2, 0, i)
            ),
        ),
        out_shape=jax.ShapeDtypeStruct((count // own, 2, own, D), LOW),
        compiler_params=pltpu.CompilerParams(vmem_limit_bytes=ROOM),
        cost_estimate=SHORT,
    )(core, *mine, *other, *rights)


def weight_kernel(parts, outs, *refs):
    lefts, rights, out_ref = refs[:parts], refs[parts:-1], refs[-1]
    width = out_ref.shape[1] // outs
    for j in range(outs):
        total = None
        for i, left in enumerate(lefts):
            part = over_tokens(left[...], rights[i * outs + j][...])
            total = part if total is None else total + part
        out_ref[:, j * width : (j + 1) * width] = total.astype(out_ref.dtype)


def weight_grads(lefts, rights):
    parts, outs = len(lefts), len(rights[0])
    flat = [r for row in rights for r in row]
    rows, tile = lefts[0].shape[1], 512
    width = sum(r.shape[1] for r in rights[0])
    return pl.pallas_call(
        functools.partial(weight_kernel, parts, outs),
        grid=(rows // tile,),
        in_specs=[pl.BlockSpec((a.shape[0], tile), lambda i: (0, i)) for a in lefts]
        + [pl.BlockSpec(r.shape, lambda i: (0, 0), pipeline_mode=pl.Buffered(1)) for r in flat],
        out_specs=pl.BlockSpec((tile, width), lambda i: (i, 0)),
        out_shape=jax.ShapeDtypeStruct((rows, width), LOW),
        compiler_params=pltpu.CompilerParams(vmem_limit_bytes=ROOM),
        cost_estimate=SHORT,
    )(*lefts, *flat)


def prep_feed_kernel(nc, nh, w_ref, out_ref):
    width = out_ref.shape[2]
    for c in range(nc):
        for h in range(nh):
            at = (c * nh + h) * width
            out_ref[h * nc + c] = w_ref[:, at : at + width].astype(LOW)


def prep_feed(sizes, w, first):
    ny, nc, nh, _ = sizes
    rows, block = w.shape[0], FF // ny
    return pl.pallas_call(
        functools.partial(prep_feed_kernel, nc, nh),
        grid=(ny,),
        in_specs=[pl.BlockSpec((rows, block), lambda i: (0, first // block + i))],
        out_specs=pl.BlockSpec((nh * nc, rows, block // (nh * nc)), lambda i: (0, 0, i)),
        out_shape=jax.ShapeDtypeStruct((nh * nc, rows, FF // (nh * nc)), LOW),
        compiler_params=pltpu.CompilerParams(vmem_limit_bytes=ROOM),
        cost_estimate=SHORT,
    )(w)


def prep_conv_kernel(sizes, w_ref, out_ref):
    ny, nc, nh, nl = sizes
    rows = w_ref.shape[0]
    for yc in range(ny * nc):
        for k in range(nl):
            parts = [
                w_ref[:, ((yc * nh + h) * nl + k) * rows : ((yc * nh + h) * nl + k + 1) * rows]
                for h in range(nh)
            ]
            out_ref[yc * nl + k, 0] = jnp.concatenate(parts, 1).astype(LOW)


def prep_conv(sizes, w):
    ny, nc, nh, nl = sizes
    rows = w.shape[0]
    shape = (ny * nc * nl, 3, rows, nh * rows)
    return pl.pallas_call(
        functools.partial(prep_conv_kernel, sizes),
        grid=(3,),
        in_specs=[pl.BlockSpec((rows, D), lambda i: (0, i))],
        out_specs=pl.BlockSpec((shape[0], 1) + shape[2:], lambda i: (0, i, 0, 0)),
        out_shape=jax.ShapeDtypeStruct(shape, LOW),
        compiler_params=pltpu.CompilerParams(vmem_limit_bytes=ROOM),
        cost_estimate=SHORT,
    )(w)


def fold(values):
    rows, cols = values.shape
    total = values[:, :128]
    for k in range(1, cols // 128):
        total = total + values[:, 128 * k : 128 * (k + 1)]
    out = total[:8]
    for k in range(1, rows // 8):
        out = out + total[8 * k : 8 * (k + 1)]
    return out


def adam_step(first, grad, w_ref, m_ref, v_ref, grad_ref, nm_ref, nv_ref, dir_ref, sum_ref):
    weight = w_ref[...]
    new_m, new_v, direction = adam_direction(weight, grad, m_ref[...], v_ref[...])
    grad_ref[...] = grad
    nm_ref[...] = new_m
    nv_ref[...] = new_v
    dir_ref[...] = direction

    @pl.when(first)
    def _():
        sum_ref[...] = jnp.zeros_like(sum_ref)

    sum_ref[0, 0] += fold(weight * weight)
    sum_ref[0, 1] += fold(direction * direction)


def adam_gate_kernel(w_ref, m_ref, v_ref, got_ref, *refs):
    grad = jnp.concatenate([got_ref[h, 0] for h in range(got_ref.shape[0])], 1).astype(WIDE)
    adam_step(pl.program_id(0) == 0, grad, w_ref, m_ref, v_ref, *refs[-5:])


def adam_gate(sizes, w, m, v, got, kind, done=()):
    ny, nc, nh, _ = sizes
    rows = w.shape[0]
    part = got.shape[2] // (2 * ny)
    width = nh * part
    first = 4 * D + kind * FF
    column = pl.BlockSpec((rows, width), lambda b: (0, first // width + b))
    like = jax.ShapeDtypeStruct(w.shape, WIDE)
    return pl.pallas_call(
        adam_gate_kernel,
        grid=(ny * nc,),
        in_specs=[column] * 3
        + [pl.BlockSpec((nh, 1, rows, part), lambda b: (0, b % nc, 0, kind * ny + b // nc))]
        + [pl.BlockSpec(memory_space=pl.ANY) for _ in done],
        out_specs=[column] * 4 + [pl.BlockSpec((1, 2, 8, 128), lambda b: (0, 0, 0, 0))],
        out_shape=[like] * 4 + [jax.ShapeDtypeStruct((1, 2, 8, 128), WIDE)],
        input_output_aliases={4 + k: k for k in range(len(done))},
        compiler_params=pltpu.CompilerParams(vmem_limit_bytes=ROOM),
        cost_estimate=SHORT,
    )(w, m, v, got.reshape(nh, nc, rows, -1), *done)


def adam_plain_kernel(w_ref, m_ref, v_ref, g_ref, *refs):
    adam_step(pl.program_id(1) == 0, g_ref[...].astype(WIDE), w_ref, m_ref, v_ref, *refs[-5:])


def adam_columns(w, m, v, grad, first, kinds, done=()):
    rows = w.shape[0]
    width = 1024
    blocks = grad.shape[1] // (kinds * width)
    column = pl.BlockSpec((rows, width), lambda k, b: (0, first // width + k * blocks + b))
    like = jax.ShapeDtypeStruct(w.shape, WIDE)
    return pl.pallas_call(
        adam_plain_kernel,
        grid=(kinds, blocks),
        in_specs=[column] * 3
        + [pl.BlockSpec((rows, width), lambda k, b: (0, k * blocks + b))]
        + [pl.BlockSpec(memory_space=pl.ANY) for _ in done],
        out_specs=[column] * 4 + [pl.BlockSpec((1, 2, 8, 128), lambda k, b: (k, 0, 0, 0))],
        out_shape=[like] * 4 + [jax.ShapeDtypeStruct((kinds, 2, 8, 128), WIDE)],
        input_output_aliases={4 + k: k for k in range(len(done))},
        compiler_params=pltpu.CompilerParams(vmem_limit_bytes=ROOM),
        cost_estimate=SHORT,
    )(w, m, v, grad, *done)


def adam_down(w, m, v, grad):
    rows = 64
    block = pl.BlockSpec((rows, D), lambda k, i: (i, 0))
    like = jax.ShapeDtypeStruct(w.shape, WIDE)
    return pl.pallas_call(
        adam_plain_kernel,
        grid=(1, w.shape[0] // rows),
        in_specs=[block] * 4,
        out_specs=[block] * 4 + [pl.BlockSpec((1, 2, 8, 128), lambda k, i: (0, 0, 0, 0))],
        out_shape=[like] * 4 + [jax.ShapeDtypeStruct((1, 2, 8, 128), WIDE)],
        compiler_params=pltpu.CompilerParams(vmem_limit_bytes=ROOM),
        cost_estimate=SHORT,
    )(w, m, v, grad)


def adam_first_kernel(sizes, w_ref, m_ref, v_ref, got_ref, *refs):
    ny, nc, nh, nl = sizes
    rows = w_ref.shape[0]
    parts = []
    for yc in range(ny * nc):
        for h in range(nh):
            for k in range(nl):
                parts.append(got_ref[yc * nl + k, 0, :, h * rows : (h + 1) * rows])
    grad = jnp.concatenate(parts, 1).astype(WIDE)
    adam_step(pl.program_id(0) == 0, grad, w_ref, m_ref, v_ref, *refs[-5:])


def adam_first(sizes, w, m, v, got, done=()):
    rows = w.shape[0]
    column = pl.BlockSpec((rows, D), lambda i: (0, i))
    like = jax.ShapeDtypeStruct(w.shape, WIDE)
    return pl.pallas_call(
        functools.partial(adam_first_kernel, sizes),
        grid=(3,),
        in_specs=[column] * 3
        + [pl.BlockSpec((got.shape[0], 1) + got.shape[2:], lambda i: (0, i, 0, 0))]
        + [pl.BlockSpec(memory_space=pl.ANY) for _ in done],
        out_specs=[column] * 4 + [pl.BlockSpec((1, 2, 8, 128), lambda i: (0, 0, 0, 0))],
        out_shape=[like] * 4 + [jax.ShapeDtypeStruct((1, 2, 8, 128), WIDE)],
        input_output_aliases={4 + k: k for k in range(len(done))},
        compiler_params=pltpu.CompilerParams(vmem_limit_bytes=ROOM),
        cost_estimate=SHORT,
    )(w, m, v, got, *done)


def step_kernel(ratio_ref, w_ref, dir_ref, out_ref):
    block = pl.program_id(0)
    piece = jnp.where(block < 3, 0, jnp.where(block < 4, 1, jnp.where(block < 4 + FF // D, 2, 3)))
    out_ref[...] = w_ref[...] + dir_ref[...] * ratio_ref[piece]


def stepped(ratio, w, direction):
    rows, cols = w.shape
    column = pl.BlockSpec((rows, D), lambda b, r: (0, b))
    return pl.pallas_call(
        step_kernel,
        grid_spec=pltpu.PrefetchScalarGridSpec(
            num_scalar_prefetch=1, grid=(cols // D,), in_specs=[column] * 2, out_specs=column
        ),
        out_shape=jax.ShapeDtypeStruct(w.shape, WIDE),
        compiler_params=pltpu.CompilerParams(vmem_limit_bytes=ROOM),
        cost_estimate=SHORT,
    )(ratio, w, direction)


def local(
    inputs,
    out_grad,
    segments,
    w_in,
    w_down,
    conv_taps,
    norm_gains,
    m_in,
    m_down,
    m_taps,
    m_gains,
    v_in,
    v_down,
    v_taps,
    v_gains,
):
    sizes = tuple(lax.axis_size(a) for a in AXES)
    ny, nc, nh, nl = sizes
    yi, ci, hi, li = (lax.axis_index(a) for a in AXES)
    own = inputs.shape[0] * inputs.shape[1]
    rows = w_in.shape[0]
    wide_rows = w_down.shape[0]
    channels = nh * rows
    span = ny * nc * own
    conv_total = nl * span

    def feed_order(a):
        return a.reshape(own, ny, nc, nh, nl, rows).transpose(0, 1, 4, 3, 2, 5).reshape(own, D)

    def from_feed_order(a):
        return a.reshape(own, ny, nl, nh, nc, rows).transpose(0, 1, 4, 3, 2, 5).reshape(own, D)

    def conv_order(a):
        return rolled(a.reshape(own, ny * nc, nh, -1).swapaxes(1, 2), "h", 1, 1).reshape(own, D)

    def from_conv_order(a):
        return rolled(a.reshape(own, nh, ny * nc, -1), "h", 1, -1).swapaxes(1, 2).reshape(own, D)

    def near(value, axes, first=1, last=None):
        last = lax.axis_size(axes) if last is None else last
        return [turned(value, axes, -k) for k in range(first, last)]

    def ring(value, axis):
        pieces = [value]
        for _ in range(1, lax.axis_size(axis)):
            pieces.append(turned(pieces[-1], axis, -1))
        return pieces

    def ring_sum(blocks, axis):
        n = lax.axis_size(axis)
        passed = blocks[n - 1]
        for k in range(n - 2, -1, -1):
            passed = turned(passed.astype(LOW), axis, 1).astype(WIDE) + blocks[k].astype(WIDE)
        return passed

    def with_core(pieces):
        mine = jnp.concatenate(pieces, 0)
        return mine, turned(mine, "c", 1)

    def scatter(other, mine, axes):
        both = turned(other, "c", 1)
        both = (mine() + both.astype(WIDE)).reshape(-1, own, D)
        sent = [turned(both[k].astype(LOW), axes, k) for k in range(1, both.shape[0])]
        return both[0], sent

    def total(first, sent):
        for s in sent:
            first = first + s.astype(WIDE)
        return first

    def out_order(a):
        return rolled(a, "h", 0, -1)

    note = jnp.concatenate(
        [norm_gains.reshape(-1), conv_taps.reshape(-1), segments.reshape(-1).astype(WIDE)]
    )
    low_o = w_in[:, 3 * D : 4 * D].astype(LOW)
    notes, p_cols, low_o = tied(spread_to(note, AXES), prep_conv(sizes, w_in), low_o)
    o_pieces = [low_o] + near(low_o, "h")
    notes = notes.reshape(sizes + (-1,))
    gains = notes[..., : 2 * rows].reshape(D, 2).astype(LOW).astype(WIDE)
    gain_one = gains[:, 0]
    gain_two = gains[:, 1]
    of_group = picked(picked(picked(notes, li, 3), ci, 1), yi, 0)
    taps = of_group[:, 2 * rows : 5 * rows].reshape(channels, TAPS).astype(LOW).astype(WIDE)
    ids = picked(notes[..., 5 * rows :], hi, 2).transpose(2, 0, 1, 3).reshape(nl, span)

    def as_rows(a):
        return a.reshape(-1, a.shape[-1])

    grad_low = out_grad.reshape(own, D)
    grad_top = grad_low.astype(WIDE)
    down = lax.all_gather(w_down.astype(LOW), FEED_COPIES, axis=0, tiled=True)
    values = inputs.reshape(own, D).astype(WIDE)
    norm_one, scale_one = norm_forward(values, gain_one)
    low_one = conv_order(norm_one.astype(LOW))
    cols_p, gate_cols, low_one, *o_pieces = tied(
        exchanged(p_cols, CONV), prep_feed(sizes, w_in, 4 * D), low_one, *o_pieces
    )
    h_pieces = [low_one] + near(low_one, LINES)
    gate_cols, up_cols, cols_p, down, h_pieces[1] = tied(
        exchanged(gate_cols, FEED), prep_feed(sizes, w_in, 4 * D + FF), cols_p, down, h_pieces[1]
    )
    mine, other = with_core(h_pieces)
    gate_w = lax.all_gather(as_rows(gate_cols), FEED_COPIES, axis=0, tiled=True)
    up_cols, cols_p = tied(exchanged(up_cols, FEED), cols_p)
    up_w = lax.all_gather(as_rows(up_cols), FEED_COPIES, axis=0, tiled=True)
    o_w = placed(o_pieces, "h").reshape(channels, D)
    pieces = [cols_p.swapaxes(1, 2).reshape(-1, 3 * channels)]
    for k in range(1, nh):
        piece = turned(pieces[-1], "h", -1)
        pieces.append(piece)
    pieces[-1], gate_w = tied(pieces[-1], gate_w)
    p_w = jnp.concatenate(pieces, 0)

    line = li * ny + yi
    h_one = interleaved(jnp.stack([line, ci]), mine, other, own).reshape(conv_total, D)
    bcx = times(h_one, p_w).reshape(nl, span, 3 * channels)
    b_part = bcx[:, :, :channels]
    c_part = bcx[:, :, channels : 2 * channels]
    x_part = bcx[:, :, 2 * channels :]
    mixed_in = b_part * x_part
    extended = jnp.pad(mixed_in, ((0, 0), (2, 0), (0, 0)))
    ext_ids = jnp.pad(ids, ((0, 0), (2, 0)), constant_values=-1.0)
    keeps = []
    conv = jnp.zeros((nl, span, channels), WIDE)
    for lag in range(TAPS):
        keep = (ext_ids[:, 2 - lag : 2 - lag + span] == ids).astype(WIDE)[:, :, None]
        keeps.append(keep)
        conv = conv + taps[:, lag] * extended[:, 2 - lag : 2 - lag + span] * keep
    y_mix = (c_part * conv).astype(LOW)

    def by_core(value):
        parts = rolled(value.reshape(ny * nl, nc, own, -1), LINES, 0, 1)
        return [picked(parts, (ci + k) % nc, 1).reshape(ny * nl * own, -1) for k in range(nc)]

    y_mine, y_other = by_core(y_mix)
    both, sent = scatter(times(y_other, o_w).astype(LOW), lambda: times(y_mine, o_w), LINES)
    both, up_w, grad_low = tied(both, up_w, grad_low)
    e_all = lax.all_gather(grad_low, FEED, axis=0)
    middle = values + total(both, sent)

    norm_two, scale_two = norm_forward(middle, gain_two)
    low_two = feed_order(norm_two.astype(LOW))
    h_mine = assembled(hi, [low_two] + near(low_two, "h"))
    h_other = turned(h_mine, "c", 1)
    e_all = e_all.reshape(nh, nc, own, D)
    core = ci.reshape(1).astype(jnp.int32)
    hid_mine, dg_mine, du_mine = feed(core, h_mine, e_all, gate_w, up_w, down)
    hid_other, dg_other, du_other = feed(1 - core, h_other, e_all, gate_w, up_w, down)
    def summed(part, axes):
        return lax.psum_scatter(part, axes, scatter_dimension=0, tiled=True)

    d_h_two = both_cores(core, [dg_mine, du_mine], [dg_other, du_other], [gate_w, up_w], own, True)
    d_h_two, h_mine = tied(d_h_two, h_mine)
    d_h_two = summed(d_h_two.reshape(-1, D), FEED).astype(WIDE)
    part_feed = weight_grads([h_mine, h_other], [[dg_mine, du_mine], [dg_other, du_other]])
    part_feed, hid_mine = tied(part_feed, hid_mine)
    part_down = down_grads(core, hid_mine, hid_other, e_all)
    out_part = both_cores(core, [hid_mine], [hid_other], [down], own, False)
    d_h_two, part_down, part_feed, out_part = tied(d_h_two, part_down, part_feed, out_part)
    out_sum = summed(out_part.reshape(-1, D), FEED)
    d_middle, d_gain_two = norm_backward(middle, scale_two, gain_two, from_feed_order(d_h_two))
    d_middle = d_middle + grad_top

    low_branch = d_middle.astype(LOW)
    do_mine, do_other = with_core([low_branch] + near(low_branch, LINES))
    do_mine, do_other, part_feed = tied(do_mine, do_other, part_feed)
    got_feed = summed(part_feed, FEED_COPIES)
    part_o = over_tokens(y_mine, do_mine) + over_tokens(y_other, do_other)
    part_o = rolled(part_o.reshape(nh, rows, D), "h", 0, 1)
    part_o = part_o.astype(LOW)
    d_mix = jnp.zeros((ny * nl, nc, own, channels), WIDE)
    for k, part in enumerate((do_mine, do_other)):
        part = rolled(times_wide(part, o_w).reshape(-1, 1, own, channels), LINES, 0, -1)
        d_mix = lax.dynamic_update_slice(d_mix, part, (0, (ci + k) % nc, 0, 0))
    d_mix = d_mix.reshape(nl, span, channels)
    d_c = d_mix * conv
    d_conv = d_mix * c_part
    d_extended = jnp.zeros((nl, span + 2, channels), WIDE)
    tap_grads = []
    for lag in range(TAPS):
        counted = d_conv * keeps[lag]
        tap_grads.append(jnp.sum(counted * extended[:, 2 - lag : 2 - lag + span], axis=(0, 1)))
        d_extended = d_extended + jnp.pad(taps[:, lag] * counted, ((0, 0), (2 - lag, lag), (0, 0)))
    d_mixed_in = d_extended[:, 2:]
    d_bcx = jnp.concatenate([d_mixed_in * x_part, d_c, d_mixed_in * b_part], 2).astype(LOW)

    part_p = weight_grads([h_one], [[d_bcx.reshape(conv_total, -1)]]).reshape(nh, -1, 3 * channels)
    part_p, part_o, d_bcx, part_down, out_sum = tied(part_p, part_o, d_bcx, part_down, out_sum)
    grad_down = summed(part_down, FEED_COPIES)
    db_mine, db_other = by_core(d_bcx)
    pass_p, pass_o = part_p[nh - 1], part_o[nh - 1]
    for k in range(nh - 2, -1, -1):
        pass_p, pass_o = turned(pass_p, "h", 1), turned(pass_o, "h", 1)
        if k == nh - 2:
            other = back([db_other], p_w, LOW)
            other, db_mine = tied(other, db_mine)
            both, sent = scatter(other, lambda: back([db_mine], p_w, WIDE), LINES)
            pass_p, pass_o, both = tied(pass_p, pass_o, both)
        if k == 0:
            pass_p, pass_o = tied(pass_p, pass_o)
        pass_p = pass_p.astype(WIDE) + part_p[k].astype(WIDE)
        pass_o = pass_o.astype(WIDE) + part_o[k].astype(WIDE)
        if k:
            pass_p, pass_o = pass_p.astype(LOW), pass_o.astype(LOW)
    grad_o = pass_o
    part_p = pass_p.astype(LOW).reshape(ny * nc * nl, rows, 3, channels).swapaxes(1, 2)
    got_feed, part_p = tied(got_feed, part_p)
    got_feed = exchanged(got_feed.reshape(nh * nc, rows, -1), FEED)
    *done, sums_o = adam_columns(w_in, m_in, v_in, grad_o, 3 * D, 1)
    got_feed, part_p, sums_o = tied(got_feed, part_p, sums_o)
    got_p, *sent = tied(exchanged(part_p, CONV), *sent)
    d_h_one = total(both, sent)
    d_values, d_gain_one = norm_backward(values, scale_one, gain_one, from_conv_order(d_h_one))
    input_grad = (d_values + d_middle).reshape(inputs.shape)

    tap_terms = jnp.stack(tap_grads, 1).reshape(1, 1, nh, 1, rows, TAPS)
    tap_terms = lax.dynamic_update_slice(
        jnp.zeros(sizes + (rows, TAPS), WIDE), tap_terms, (yi, ci, 0, li, 0, 0)
    )
    gain_terms = jnp.stack([d_gain_one, d_gain_two], 1).reshape(sizes + (rows, 2))
    terms = jnp.concatenate([tap_terms, gain_terms], -1).reshape(-1, rows, TAPS + 2)
    terms = exchanged(terms, AXES)
    *done, sums_gate = adam_gate(sizes, w_in, m_in, v_in, got_feed, 0, done)
    *done, sums_up = adam_gate(sizes, w_in, m_in, v_in, got_feed, 1, done)
    *done, sums_p = adam_first(sizes, w_in, m_in, v_in, got_p, done)
    grad_down, sums_up = tied(grad_down, sums_up)
    grad_down, new_m_down, new_v_down, dir_down, sums_down = adam_down(w_down, m_down, v_down, grad_down)
    grad_in, new_m_in, new_v_in, dir_in = done
    block_out = (middle + out_sum.astype(WIDE)).astype(LOW).reshape(inputs.shape)
    terms = jnp.sum(terms, axis=0)
    grad_taps, grad_gains = terms[:, :TAPS], terms[:, TAPS:]
    new_m_taps, new_v_taps, dir_taps = adam_direction(conv_taps, grad_taps, m_taps, v_taps)
    new_m_gains, new_v_gains, dir_gains = adam_direction(norm_gains, grad_gains, m_gains, v_gains)

    def lanes(a):
        return jnp.pad(jnp.sum(a * a, axis=0), (0, 128 - a.shape[1]))

    def small(taps_like, gains_like):
        return jnp.stack(
            [lanes(taps_like), lanes(gains_like[:, :1]), lanes(gains_like[:, 1:])], 0
        )

    sums = jnp.concatenate(
        [
            jnp.sum(jnp.concatenate([sums_p, sums_o, sums_gate, sums_up, sums_down], 0), axis=2),
            jnp.stack([small(conv_taps, norm_gains), small(dir_taps, dir_gains)], 1),
        ],
        0,
    )
    lamb_norms = jnp.sqrt(jnp.sum(spread_to(sums, AXES), axis=(0, 3)).T)
    ratio = -RATE * lamb_norms[0] / (lamb_norms[1] + 1e-06)
    new_w_in = stepped(ratio[:4], w_in, dir_in)
    new_w_down = w_down + dir_down * ratio[4]
    new_w_taps = conv_taps + dir_taps * ratio[5]
    new_w_gains = norm_gains + dir_gains * ratio[6:][None, :]
    return (
        block_out,
        input_grad,
        grad_in,
        grad_down,
        grad_taps,
        grad_gains,
        new_m_in,
        new_m_down,
        new_m_taps,
        new_m_gains,
        new_v_in,
        new_v_down,
        new_v_taps,
        new_v_gains,
        new_w_in,
        new_w_down,
        new_w_taps,
        new_w_gains,
        lamb_norms,
    )


def solution(mesh):
    seq, shard = mesh.shape["seq"], mesh.shape["shard"]
    grid = Mesh(mesh.devices.reshape(seq // 2, 2, 4, shard // 4), AXES)
    tokens = P(("h", "l"), ("y", "c"), None)
    weights = P(AXES, None)
    return jax.shard_map(
        local,
        mesh=grid,
        in_specs=(tokens, tokens, P(("h", "l"), ("y", "c"))) + (weights,) * 12,
        out_specs=(tokens, tokens) + (weights,) * 16 + (P(),),
        check_vma=False,
    )
```

```python
import functools

import jax
import jax.numpy as jnp
import numpy as np
from jax import lax
from jax.experimental import pallas as pl
from jax.experimental.pallas import tpu as pltpu
from jax.sharding import Mesh
from jax.sharding import PartitionSpec as P

D = 2048
FF = 8192
TAPS = 3
STEP = 4


EPS_NORM = 1e-05
BETA_ONE = 0.9
BETA_TWO = 0.999
EPS_ADAM = 1e-08
DECAY = 0.01
RATE = 0.3

AXES = ("y", "c", "h", "l")
FEED = ("h", "c")
FEED_COPIES = ("y", "l")
CONV = ("y", "c", "l")
LINES = ("l", "y")
LOW = jnp.bfloat16
WIDE = jnp.float32
ROOM = 56 * 1024 * 1024
SHORT = pl.CostEstimate(flops=1024, bytes_accessed=1024, transcendentals=0)


def turned(value, axes, steps):
    n = lax.axis_size(axes)
    names = (axes,) if isinstance(axes, str) else axes
    ordered = tuple(a for a in AXES if a in names)
    where = np.arange(n).reshape([lax.axis_size(a) for a in ordered])
    where = where.transpose([ordered.index(a) for a in names]).reshape(-1)
    pairs = [(int(where[i]), int(where[(i + steps) % n])) for i in range(n)]
    return lax.ppermute(value, ordered if len(names) > 1 else axes, pairs)


def tied(*values):
    return lax.optimization_barrier(values)


def picked(value, index, dim):
    return lax.dynamic_index_in_dim(value, index, dim, keepdims=False)


def exchanged(value, axes):
    return lax.all_to_all(value, axes, 0, 0, tiled=True)


def spread_to(value, axes):
    return exchanged(jnp.broadcast_to(value[None], (lax.axis_size(axes),) + value.shape), axes)


def rolled(value, axis, dim, sign):
    n, me = lax.axis_size(axis), lax.axis_index(axis)
    twice = jnp.concatenate([value, value], dim)
    return lax.dynamic_slice_in_dim(twice, (sign * me) % n, n, dim)


def placed(pieces, axis):
    n, me = len(pieces), lax.axis_index(axis)
    out = jnp.zeros((n,) + pieces[0].shape, pieces[0].dtype)
    for k, piece in enumerate(pieces):
        out = lax.dynamic_update_slice(
            out, piece[None], ((me + k) % n,) + (0,) * piece.ndim
        )
    return out


def norm_forward(values, gain):
    scale = lax.rsqrt(jnp.mean(values * values, axis=-1, keepdims=True) + EPS_NORM)
    return (values * scale * gain, scale)


def norm_backward(values, scale, gain, grad):
    along = grad * gain
    inner = jnp.mean(along * values, axis=-1, keepdims=True)
    d_values = scale * along - scale * scale * scale * values * inner
    d_gain = jnp.sum(grad * values * scale, axis=0)
    return (d_values, d_gain)


def times(left, right):
    return jnp.dot(left, right, preferred_element_type=WIDE)


def times_wide(left, right):
    return lax.dot_general(
        left, right, (((1,), (1,)), ((), ())), preferred_element_type=WIDE
    )


def over_tokens(left, right):
    return lax.dot_general(
        left, right, (((0,), (0,)), ((), ())), preferred_element_type=WIDE
    )


def adam_direction(weight, grad, first, second):
    new_first = BETA_ONE * first + (1.0 - BETA_ONE) * grad
    new_second = BETA_TWO * second + (1.0 - BETA_TWO) * grad * grad
    first_hat = new_first / (1.0 - BETA_ONE**STEP)
    second_hat = new_second / (1.0 - BETA_TWO**STEP)
    direction = first_hat / (jnp.sqrt(second_hat) + EPS_ADAM) + DECAY * weight
    return (new_first, new_second, direction)


def assembled_kernel(me_ref, *refs):
    out_ref, n = refs[-1], len(refs) - 1
    for k in range(n):
        out_ref[pl.ds((me_ref[0] + k) % n, 1)] = refs[k][...][None]


def assembled(me, pieces):
    rows, cols = pieces[0].shape
    n = len(pieces)
    out = pl.pallas_call(
        assembled_kernel,
        in_specs=[pl.BlockSpec(memory_space=pltpu.SMEM)]
        + [pl.BlockSpec(memory_space=pltpu.VMEM) for _ in pieces],
        out_specs=pl.BlockSpec(memory_space=pltpu.VMEM),
        out_shape=jax.ShapeDtypeStruct((n, rows, cols), LOW),
        compiler_params=pltpu.CompilerParams(vmem_limit_bytes=ROOM),
        cost_estimate=SHORT,
    )(me.reshape(1).astype(jnp.int32), *pieces)
    return out.reshape(n * rows, cols)


def interleaved_kernel(place_ref, mine_ref, other_ref, out_ref):
    out_ref[0, pl.ds(place_ref[1], 1)] = mine_ref[...][None]
    out_ref[0, pl.ds(1 - place_ref[1], 1)] = other_ref[...][None]


def interleaved(place, mine, other, own):
    n, cols = mine.shape[0] // own, mine.shape[1]
    block = pl.BlockSpec((own, cols), lambda i, p: (i, 0))
    return pl.pallas_call(
        interleaved_kernel,
        grid_spec=pltpu.PrefetchScalarGridSpec(
            num_scalar_prefetch=1,
            grid=(n,),
            in_specs=[block, block],
            out_specs=pl.BlockSpec((1, 2, own, cols), lambda i, p: ((p[0] + i) % n, 0, 0, 0)),
        ),
        out_shape=jax.ShapeDtypeStruct((n, 2, own, cols), mine.dtype),
        compiler_params=pltpu.CompilerParams(vmem_limit_bytes=ROOM),
        cost_estimate=SHORT,
    )(place.astype(jnp.int32), mine, other)


def feed_kernel(c_ref, h_ref, e_ref, g_ref, u_ref, d_ref, hid_ref, dg_ref, du_ref):
    step = 256
    grads = e_ref[...].reshape(h_ref.shape)
    for j in range(h_ref.shape[0] // step):
        at = slice(j * step, (j + 1) * step)
        gate = times(h_ref[at, :], g_ref[...])
        up = times(h_ref[at, :], u_ref[...])
        d_hidden = times_wide(grads[at, :], d_ref[...])
        sig = jax.nn.sigmoid(gate)
        activated = gate * sig
        hid_ref[at, :] = (activated * up).astype(LOW)
        dg_ref[at, :] = (d_hidden * up * (sig * (1.0 + gate * (1.0 - sig)))).astype(LOW)
        du_ref[at, :] = (d_hidden * activated).astype(LOW)


def feed(core, h, e, gate, up, down):
    count, features = h.shape[0], down.shape[0]
    tile = 256
    made = pl.BlockSpec((count, tile), lambda i, c: (0, i))
    return pl.pallas_call(
        feed_kernel,
        grid_spec=pltpu.PrefetchScalarGridSpec(
            num_scalar_prefetch=1,
            grid=(features // tile,),
            in_specs=[
                pl.BlockSpec((count, D), lambda i, c: (0, 0), pipeline_mode=pl.Buffered(1)),
                pl.BlockSpec(
                    (e.shape[0], 1) + e.shape[2:],
                    lambda i, c: (0, c[0], 0, 0),
                    pipeline_mode=pl.Buffered(1),
                ),
                pl.BlockSpec((D, tile), lambda i, c: (0, i)),
                pl.BlockSpec((D, tile), lambda i, c: (0, i)),
                pl.BlockSpec((tile, D), lambda i, c: (i, 0)),
            ],
            out_specs=[made] * 3,
        ),
        out_shape=[jax.ShapeDtypeStruct((count, features), LOW)] * 3,
        compiler_params=pltpu.CompilerParams(vmem_limit_bytes=ROOM),
        cost_estimate=SHORT,
    )(core, h, e, gate, up, down)


def down_kernel(c_ref, mine_ref, other_ref, mine_e_ref, other_e_ref, out_ref):
    rows = mine_ref.shape[0]
    total = over_tokens(mine_ref[...], mine_e_ref[...].reshape(rows, -1))
    total += over_tokens(other_ref[...], other_e_ref[...].reshape(rows, -1))
    out_ref[...] = total.astype(out_ref.dtype)


def down_grads(core, mine, other, e):
    count, features = mine.shape
    tile = 512
    side = (e.shape[0], 1) + e.shape[2:]
    return pl.pallas_call(
        down_kernel,
        grid_spec=pltpu.PrefetchScalarGridSpec(
            num_scalar_prefetch=1,
            grid=(features // tile,),
            in_specs=[
                pl.BlockSpec((count, tile), lambda i, c: (0, i)),
                pl.BlockSpec((count, tile), lambda i, c: (0, i)),
                pl.BlockSpec(side, lambda i, c: (0, c[0], 0, 0), pipeline_mode=pl.Buffered(1)),
                pl.BlockSpec(side, lambda i, c: (0, 1 - c[0], 0, 0), pipeline_mode=pl.Buffered(1)),
            ],
            out_specs=pl.BlockSpec((tile, D), lambda i, c: (i, 0)),
        ),
        out_shape=jax.ShapeDtypeStruct((features, D), LOW),
        compiler_params=pltpu.CompilerParams(vmem_limit_bytes=ROOM),
        cost_estimate=SHORT,
    )(core, mine, other, e, e)


def back_kernel(pairs, *refs):
    out_ref = refs[-1]
    total = None
    for left, right in zip(refs[:pairs], refs[pairs:-1]):
        part = times_wide(left[...], right[...])
        total = part if total is None else total + part
    out_ref[...] = total.astype(out_ref.dtype)


def back(lefts, right, dtype):
    count, width = lefts[0].shape
    tile = 512
    return pl.pallas_call(
        functools.partial(back_kernel, len(lefts)),
        grid=(D // tile,),
        in_specs=[
            pl.BlockSpec(a.shape, lambda i: (0, 0), pipeline_mode=pl.Buffered(1)) for a in lefts
        ]
        + [pl.BlockSpec((tile, width), lambda i, k=k: (i, k)) for k in range(len(lefts))],
        out_specs=pl.BlockSpec((count, tile), lambda i: (0, i)),
        out_shape=jax.ShapeDtypeStruct((count, D), dtype),
        compiler_params=pltpu.CompilerParams(vmem_limit_bytes=ROOM),
        cost_estimate=SHORT,
    )(*lefts, *[right] * len(lefts))


def both_kernel(count, wide, c_ref, *refs):
    out_ref = refs[-1]
    mine, other, rights = refs[:count], refs[count : 2 * count], refs[2 * count : -1]
    product = times_wide if wide else times

    def write(lefts):
        total = None
        for left, right in zip(lefts, rights):
            part = product(left[...], right[...])
            total = part if total is None else total + part
        out_ref[...] = total.astype(out_ref.dtype).reshape(out_ref.shape)

    @pl.when(pl.program_id(0) == 0)
    def _():
        write(mine)

    @pl.when(pl.program_id(0) == 1)
    def _():
        write(other)


def both_cores(core, mine, other, rights, own, wide):
    count, width = mine[0].shape
    tile = 512
    if wide:
        blocks = [pl.BlockSpec((tile, width), lambda g, i, c: (i, 0)) for _ in rights]
    else:
        blocks = [pl.BlockSpec((width, tile), lambda g, i, c: (0, i)) for _ in rights]
    return pl.pallas_call(
        functools.partial(both_kernel, len(mine), wide),
        grid_spec=pltpu.PrefetchScalarGridSpec(
            num_scalar_prefetch=1,
            grid=(2, D // tile),
            in_specs=[
                pl.BlockSpec(a.shape, lambda g, i, c: (0, 0), pipeline_mode=pl.Buffered(1))
                for a in mine + other
            ]
            + blocks,
            out_specs=pl.BlockSpec(
                (count // own, 1, own, tile), lambda g, i, c: (0, (c[0] + g) % 2, 0, i)
            ),
        ),
        out_shape=jax.ShapeDtypeStruct((count // own, 2, own, D), LOW),
        compiler_params=pltpu.CompilerParams(vmem_limit_bytes=ROOM),
        cost_estimate=SHORT,
    )(core, *mine, *other, *rights)


def weight_kernel(parts, outs, *refs):
    lefts, rights, out_ref = refs[:parts], refs[parts:-1], refs[-1]
    width = out_ref.shape[1] // outs
    for j in range(outs):
        total = None
        for i, left in enumerate(lefts):
            part = over_tokens(left[...], rights[i * outs + j][...])
            total = part if total is None else total + part
        out_ref[:, j * width : (j + 1) * width] = total.astype(out_ref.dtype)


def weight_grads(lefts, rights):
    parts, outs = len(lefts), len(rights[0])
    flat = [r for row in rights for r in row]
    rows, tile = lefts[0].shape[1], 512
    width = sum(r.shape[1] for r in rights[0])
    return pl.pallas_call(
        functools.partial(weight_kernel, parts, outs),
        grid=(rows // tile,),
        in_specs=[pl.BlockSpec((a.shape[0], tile), lambda i: (0, i)) for a in lefts]
        + [pl.BlockSpec(r.shape, lambda i: (0, 0), pipeline_mode=pl.Buffered(1)) for r in flat],
        out_specs=pl.BlockSpec((tile, width), lambda i: (i, 0)),
        out_shape=jax.ShapeDtypeStruct((rows, width), LOW),
        compiler_params=pltpu.CompilerParams(vmem_limit_bytes=ROOM),
        cost_estimate=SHORT,
    )(*lefts, *flat)


def prep_feed_kernel(nc, nh, w_ref, out_ref):
    width = out_ref.shape[2]
    for c in range(nc):
        for h in range(nh):
            at = (c * nh + h) * width
            out_ref[h * nc + c] = w_ref[:, at : at + width].astype(LOW)


def prep_feed(sizes, w, first):
    ny, nc, nh, _ = sizes
    rows, block = w.shape[0], FF // ny
    return pl.pallas_call(
        functools.partial(prep_feed_kernel, nc, nh),
        grid=(ny,),
        in_specs=[pl.BlockSpec((rows, block), lambda i: (0, first // block + i))],
        out_specs=pl.BlockSpec((nh * nc, rows, block // (nh * nc)), lambda i: (0, 0, i)),
        out_shape=jax.ShapeDtypeStruct((nh * nc, rows, FF // (nh * nc)), LOW),
        compiler_params=pltpu.CompilerParams(vmem_limit_bytes=ROOM),
        cost_estimate=SHORT,
    )(w)


def prep_conv_kernel(sizes, w_ref, out_ref):
    ny, nc, nh, nl = sizes
    rows = w_ref.shape[0]
    for yc in range(ny * nc):
        for k in range(nl):
            parts = [
                w_ref[:, ((yc * nh + h) * nl + k) * rows : ((yc * nh + h) * nl + k + 1) * rows]
                for h in range(nh)
            ]
            out_ref[yc * nl + k, 0] = jnp.concatenate(parts, 1).astype(LOW)


def prep_conv(sizes, w):
    ny, nc, nh, nl = sizes
    rows = w.shape[0]
    shape = (ny * nc * nl, 3, rows, nh * rows)
    return pl.pallas_call(
        functools.partial(prep_conv_kernel, sizes),
        grid=(3,),
        in_specs=[pl.BlockSpec((rows, D), lambda i: (0, i))],
        out_specs=pl.BlockSpec((shape[0], 1) + shape[2:], lambda i: (0, i, 0, 0)),
        out_shape=jax.ShapeDtypeStruct(shape, LOW),
        compiler_params=pltpu.CompilerParams(vmem_limit_bytes=ROOM),
        cost_estimate=SHORT,
    )(w)


def fold(values):
    rows, cols = values.shape
    total = values[:, :128]
    for k in range(1, cols // 128):
        total = total + values[:, 128 * k : 128 * (k + 1)]
    out = total[:8]
    for k in range(1, rows // 8):
        out = out + total[8 * k : 8 * (k + 1)]
    return out


def adam_step(first, grad, w_ref, m_ref, v_ref, grad_ref, nm_ref, nv_ref, dir_ref, sum_ref):
    weight = w_ref[...]
    new_m, new_v, direction = adam_direction(weight, grad, m_ref[...], v_ref[...])
    grad_ref[...] = grad
    nm_ref[...] = new_m
    nv_ref[...] = new_v
    dir_ref[...] = direction

    @pl.when(first)
    def _():
        sum_ref[...] = jnp.zeros_like(sum_ref)

    sum_ref[0, 0] += fold(weight * weight)
    sum_ref[0, 1] += fold(direction * direction)


def adam_gate_kernel(w_ref, m_ref, v_ref, got_ref, *refs):
    grad = jnp.concatenate([got_ref[h, 0] for h in range(got_ref.shape[0])], 1).astype(WIDE)
    adam_step(pl.program_id(1) == 0, grad, w_ref, m_ref, v_ref, *refs[-5:])


def adam_gate(sizes, w, m, v, got, done=()):
    ny, nc, nh, _ = sizes
    rows = w.shape[0]
    part = got.shape[2] // (2 * ny)
    width = nh * part
    blocks = ny * nc
    column = pl.BlockSpec((rows, width), lambda k, b: (0, 4 * D // width + k * blocks + b))
    like = jax.ShapeDtypeStruct(w.shape, WIDE)
    return pl.pallas_call(
        adam_gate_kernel,
        grid=(2, blocks),
        in_specs=[column] * 3
        + [pl.BlockSpec((nh, 1, rows, part), lambda k, b: (0, b % nc, 0, k * ny + b // nc))]
        + [pl.BlockSpec(memory_space=pl.ANY) for _ in done],
        out_specs=[column] * 4 + [pl.BlockSpec((1, 2, 8, 128), lambda k, b: (k, 0, 0, 0))],
        out_shape=[like] * 4 + [jax.ShapeDtypeStruct((2, 2, 8, 128), WIDE)],
        input_output_aliases={4 + k: k for k in range(len(done))},
        compiler_params=pltpu.CompilerParams(vmem_limit_bytes=ROOM),
        cost_estimate=SHORT,
    )(w, m, v, got.reshape(nh, nc, rows, -1), *done)


def adam_plain_kernel(w_ref, m_ref, v_ref, g_ref, *refs):
    adam_step(pl.program_id(1) == 0, g_ref[...].astype(WIDE), w_ref, m_ref, v_ref, *refs[-5:])


def adam_columns(w, m, v, grad, first, kinds, done=()):
    rows = w.shape[0]
    width = 1024
    blocks = grad.shape[1] // (kinds * width)
    column = pl.BlockSpec((rows, width), lambda k, b: (0, first // width + k * blocks + b))
    like = jax.ShapeDtypeStruct(w.shape, WIDE)
    return pl.pallas_call(
        adam_plain_kernel,
        grid=(kinds, blocks),
        in_specs=[column] * 3
        + [pl.BlockSpec((rows, width), lambda k, b: (0, k * blocks + b))]
        + [pl.BlockSpec(memory_space=pl.ANY) for _ in done],
        out_specs=[column] * 4 + [pl.BlockSpec((1, 2, 8, 128), lambda k, b: (k, 0, 0, 0))],
        out_shape=[like] * 4 + [jax.ShapeDtypeStruct((kinds, 2, 8, 128), WIDE)],
        input_output_aliases={4 + k: k for k in range(len(done))},
        compiler_params=pltpu.CompilerParams(vmem_limit_bytes=ROOM),
        cost_estimate=SHORT,
    )(w, m, v, grad, *done)


def adam_down(w, m, v, grad):
    rows = 64
    block = pl.BlockSpec((rows, D), lambda k, i: (i, 0))
    like = jax.ShapeDtypeStruct(w.shape, WIDE)
    return pl.pallas_call(
        adam_plain_kernel,
        grid=(1, w.shape[0] // rows),
        in_specs=[block] * 4,
        out_specs=[block] * 4 + [pl.BlockSpec((1, 2, 8, 128), lambda k, i: (0, 0, 0, 0))],
        out_shape=[like] * 4 + [jax.ShapeDtypeStruct((1, 2, 8, 128), WIDE)],
        compiler_params=pltpu.CompilerParams(vmem_limit_bytes=ROOM),
        cost_estimate=SHORT,
    )(w, m, v, grad)


def adam_first_kernel(sizes, w_ref, m_ref, v_ref, got_ref, *refs):
    ny, nc, nh, nl = sizes
    rows = w_ref.shape[0]
    parts = []
    for yc in range(ny * nc):
        for h in range(nh):
            for k in range(nl):
                parts.append(got_ref[yc * nl + k, 0, :, h * rows : (h + 1) * rows])
    grad = jnp.concatenate(parts, 1).astype(WIDE)
    adam_step(pl.program_id(0) == 0, grad, w_ref, m_ref, v_ref, *refs[-5:])


def adam_first(sizes, w, m, v, got, done=()):
    rows = w.shape[0]
    column = pl.BlockSpec((rows, D), lambda i: (0, i))
    like = jax.ShapeDtypeStruct(w.shape, WIDE)
    return pl.pallas_call(
        functools.partial(adam_first_kernel, sizes),
        grid=(3,),
        in_specs=[column] * 3
        + [pl.BlockSpec((got.shape[0], 1) + got.shape[2:], lambda i: (0, i, 0, 0))]
        + [pl.BlockSpec(memory_space=pl.ANY) for _ in done],
        out_specs=[column] * 4 + [pl.BlockSpec((1, 2, 8, 128), lambda i: (0, 0, 0, 0))],
        out_shape=[like] * 4 + [jax.ShapeDtypeStruct((1, 2, 8, 128), WIDE)],
        input_output_aliases={4 + k: k for k in range(len(done))},
        compiler_params=pltpu.CompilerParams(vmem_limit_bytes=ROOM),
        cost_estimate=SHORT,
    )(w, m, v, got, *done)


def step_kernel(count, ratio_ref, w_ref, dir_ref, out_ref):
    for k in range(count):
        block = pl.program_id(0) * count + k
        piece = jnp.where(block < 3, 0, jnp.where(block < 4, 1, jnp.where(block < 4 + FF // D, 2, 3)))
        at = slice(k * D, (k + 1) * D)
        out_ref[:, at] = w_ref[:, at] + dir_ref[:, at] * ratio_ref[piece]


def stepped(ratio, w, direction):
    rows, cols = w.shape
    count = 3
    column = pl.BlockSpec((rows, count * D), lambda b, r: (0, b))
    return pl.pallas_call(
        functools.partial(step_kernel, count),
        grid_spec=pltpu.PrefetchScalarGridSpec(
            num_scalar_prefetch=1,
            grid=(cols // (count * D),),
            in_specs=[column] * 2,
            out_specs=column,
        ),
        out_shape=jax.ShapeDtypeStruct(w.shape, WIDE),
        compiler_params=pltpu.CompilerParams(vmem_limit_bytes=ROOM),
        cost_estimate=SHORT,
    )(ratio, w, direction)


def local(
    inputs,
    out_grad,
    segments,
    w_in,
    w_down,
    conv_taps,
    norm_gains,
    m_in,
    m_down,
    m_taps,
    m_gains,
    v_in,
    v_down,
    v_taps,
    v_gains,
):
    sizes = tuple(lax.axis_size(a) for a in AXES)
    ny, nc, nh, nl = sizes
    yi, ci, hi, li = (lax.axis_index(a) for a in AXES)
    own = inputs.shape[0] * inputs.shape[1]
    rows = w_in.shape[0]
    wide_rows = w_down.shape[0]
    channels = nh * rows
    span = ny * nc * own
    conv_total = nl * span

    def feed_order(a):
        return a.reshape(own, ny, nc, nh, nl, rows).transpose(0, 1, 4, 3, 2, 5).reshape(own, D)

    def from_feed_order(a):
        return a.reshape(own, ny, nl, nh, nc, rows).transpose(0, 1, 4, 3, 2, 5).reshape(own, D)

    def conv_order(a):
        return rolled(a.reshape(own, ny * nc, nh, -1).swapaxes(1, 2), "h", 1, 1).reshape(own, D)

    def from_conv_order(a):
        return rolled(a.reshape(own, nh, ny * nc, -1), "h", 1, -1).swapaxes(1, 2).reshape(own, D)

    def near(value, axes, first=1, last=None):
        last = lax.axis_size(axes) if last is None else last
        return [turned(value, axes, -k) for k in range(first, last)]

    def ring(value, axis):
        pieces = [value]
        for _ in range(1, lax.axis_size(axis)):
            pieces.append(turned(pieces[-1], axis, -1))
        return pieces

    def ring_sum(blocks, axis):
        n = lax.axis_size(axis)
        passed = blocks[n - 1]
        for k in range(n - 2, -1, -1):
            passed = turned(passed.astype(LOW), axis, 1).astype(WIDE) + blocks[k].astype(WIDE)
        return passed

    def with_core(pieces):
        mine = jnp.concatenate(pieces, 0)
        return mine, turned(mine, "c", 1)

    def scatter(other, mine, axes):
        both = turned(other, "c", 1)
        both = (mine() + both.astype(WIDE)).reshape(-1, own, D)
        sent = [turned(both[k].astype(LOW), axes, k) for k in range(1, both.shape[0])]
        return both[0], sent

    def total(first, sent):
        for s in sent:
            first = first + s.astype(WIDE)
        return first

    def out_order(a):
        return rolled(a, "h", 0, -1)

    note = jnp.concatenate(
        [norm_gains.reshape(-1), conv_taps.reshape(-1), segments.reshape(-1).astype(WIDE)]
    )
    low_o = w_in[:, 3 * D : 4 * D].astype(LOW)
    notes, p_cols, low_o = tied(spread_to(note, AXES), prep_conv(sizes, w_in), low_o)
    o_pieces = [low_o] + near(low_o, "h")
    notes = notes.reshape(sizes + (-1,))
    gains = notes[..., : 2 * rows].reshape(D, 2).astype(LOW).astype(WIDE)
    gain_one = gains[:, 0]
    gain_two = gains[:, 1]
    of_group = picked(picked(picked(notes, li, 3), ci, 1), yi, 0)
    taps = of_group[:, 2 * rows : 5 * rows].reshape(channels, TAPS).astype(LOW).astype(WIDE)
    ids = picked(notes[..., 5 * rows :], hi, 2).transpose(2, 0, 1, 3).reshape(nl, span)

    def as_rows(a):
        return a.reshape(-1, a.shape[-1])

    grad_low = out_grad.reshape(own, D)
    grad_top = grad_low.astype(WIDE)
    down = lax.all_gather(w_down.astype(LOW), FEED_COPIES, axis=0, tiled=True)
    values = inputs.reshape(own, D).astype(WIDE)
    norm_one, scale_one = norm_forward(values, gain_one)
    low_one = conv_order(norm_one.astype(LOW))
    cols_p, gate_cols, low_one, *o_pieces = tied(
        exchanged(p_cols, CONV), prep_feed(sizes, w_in, 4 * D), low_one, *o_pieces
    )
    h_pieces = [low_one] + near(low_one, LINES)
    gate_cols, up_cols, cols_p, down, h_pieces[1] = tied(
        exchanged(gate_cols, FEED), prep_feed(sizes, w_in, 4 * D + FF), cols_p, down, h_pieces[1]
    )
    mine, other = with_core(h_pieces)
    gate_w = lax.all_gather(as_rows(gate_cols), FEED_COPIES, axis=0, tiled=True)
    up_cols, cols_p = tied(exchanged(up_cols, FEED), cols_p)
    up_w = lax.all_gather(as_rows(up_cols), FEED_COPIES, axis=0, tiled=True)
    o_w = placed(o_pieces, "h").reshape(channels, D)
    pieces = [cols_p.swapaxes(1, 2).reshape(-1, 3 * channels)]
    for k in range(1, nh):
        piece = turned(pieces[-1], "h", -1)
        pieces.append(piece)
    pieces[-1], gate_w = tied(pieces[-1], gate_w)
    p_w = jnp.concatenate(pieces, 0)

    line = li * ny + yi
    h_one = interleaved(jnp.stack([line, ci]), mine, other, own).reshape(conv_total, D)
    bcx = times(h_one, p_w).reshape(nl, span, 3 * channels)
    b_part = bcx[:, :, :channels]
    c_part = bcx[:, :, channels : 2 * channels]
    x_part = bcx[:, :, 2 * channels :]
    mixed_in = b_part * x_part
    extended = jnp.pad(mixed_in, ((0, 0), (2, 0), (0, 0)))
    ext_ids = jnp.pad(ids, ((0, 0), (2, 0)), constant_values=-1.0)
    keeps = []
    conv = jnp.zeros((nl, span, channels), WIDE)
    for lag in range(TAPS):
        keep = (ext_ids[:, 2 - lag : 2 - lag + span] == ids).astype(WIDE)[:, :, None]
        keeps.append(keep)
        conv = conv + taps[:, lag] * extended[:, 2 - lag : 2 - lag + span] * keep
    y_mix = (c_part * conv).astype(LOW)

    def by_core(value):
        parts = rolled(value.reshape(ny * nl, nc, own, -1), LINES, 0, 1)
        return [picked(parts, (ci + k) % nc, 1).reshape(ny * nl * own, -1) for k in range(nc)]

    y_mine, y_other = by_core(y_mix)
    both, sent = scatter(times(y_other, o_w).astype(LOW), lambda: times(y_mine, o_w), LINES)
    both, up_w, grad_low = tied(both, up_w, grad_low)
    e_all = lax.all_gather(grad_low, FEED, axis=0)
    middle = values + total(both, sent)

    norm_two, scale_two = norm_forward(middle, gain_two)
    low_two = feed_order(norm_two.astype(LOW))
    h_mine = assembled(hi, [low_two] + near(low_two, "h"))
    h_other = turned(h_mine, "c", 1)
    e_all = e_all.reshape(nh, nc, own, D)
    core = ci.reshape(1).astype(jnp.int32)
    hid_mine, dg_mine, du_mine = feed(core, h_mine, e_all, gate_w, up_w, down)
    hid_other, dg_other, du_other = feed(1 - core, h_other, e_all, gate_w, up_w, down)
    def summed(part, axes):
        return lax.psum_scatter(part, axes, scatter_dimension=0, tiled=True)

    d_h_two = both_cores(core, [dg_mine, du_mine], [dg_other, du_other], [gate_w, up_w], own, True)
    d_h_two, h_mine = tied(d_h_two, h_mine)
    d_h_two = summed(d_h_two.reshape(-1, D), FEED).astype(WIDE)
    part_feed = weight_grads([h_mine, h_other], [[dg_mine, du_mine], [dg_other, du_other]])
    part_feed, hid_mine = tied(part_feed, hid_mine)
    part_down = down_grads(core, hid_mine, hid_other, e_all)
    out_part = both_cores(core, [hid_mine], [hid_other], [down], own, False)
    d_h_two, part_down, part_feed, out_part = tied(d_h_two, part_down, part_feed, out_part)
    out_sum = summed(out_part.reshape(-1, D), FEED)
    d_middle, d_gain_two = norm_backward(middle, scale_two, gain_two, from_feed_order(d_h_two))
    d_middle = d_middle + grad_top

    low_branch = d_middle.astype(LOW)
    do_mine, do_other = with_core([low_branch] + near(low_branch, LINES))
    do_mine, do_other, part_feed = tied(do_mine, do_other, part_feed)
    got_feed = summed(part_feed, FEED_COPIES)
    part_o = over_tokens(y_mine, do_mine) + over_tokens(y_other, do_other)
    part_o = rolled(part_o.reshape(nh, rows, D), "h", 0, 1)
    part_o = part_o.astype(LOW)
    d_mix = jnp.zeros((ny * nl, nc, own, channels), WIDE)
    for k, part in enumerate((do_mine, do_other)):
        part = rolled(times_wide(part, o_w).reshape(-1, 1, own, channels), LINES, 0, -1)
        d_mix = lax.dynamic_update_slice(d_mix, part, (0, (ci + k) % nc, 0, 0))
    d_mix = d_mix.reshape(nl, span, channels)
    d_c = d_mix * conv
    d_conv = d_mix * c_part
    d_extended = jnp.zeros((nl, span + 2, channels), WIDE)
    tap_grads = []
    for lag in range(TAPS):
        counted = d_conv * keeps[lag]
        tap_grads.append(jnp.sum(counted * extended[:, 2 - lag : 2 - lag + span], axis=(0, 1)))
        d_extended = d_extended + jnp.pad(taps[:, lag] * counted, ((0, 0), (2 - lag, lag), (0, 0)))
    d_mixed_in = d_extended[:, 2:]
    d_bcx = jnp.concatenate([d_mixed_in * x_part, d_c, d_mixed_in * b_part], 2).astype(LOW)

    part_p = weight_grads([h_one], [[d_bcx.reshape(conv_total, -1)]]).reshape(nh, -1, 3 * channels)
    part_p, part_o, d_bcx, part_down, out_sum = tied(part_p, part_o, d_bcx, part_down, out_sum)
    grad_down = summed(part_down, FEED_COPIES)
    db_mine, db_other = by_core(d_bcx)
    pass_p, pass_o = part_p[nh - 1], part_o[nh - 1]
    for k in range(nh - 2, -1, -1):
        pass_p, pass_o = turned(pass_p, "h", 1), turned(pass_o, "h", 1)
        if k == nh - 2:
            other = back([db_other], p_w, LOW)
            other, db_mine = tied(other, db_mine)
            both, sent = scatter(other, lambda: back([db_mine], p_w, WIDE), LINES)
            pass_p, pass_o, both = tied(pass_p, pass_o, both)
        if k == 0:
            pass_p, pass_o = tied(pass_p, pass_o)
        pass_p = pass_p.astype(WIDE) + part_p[k].astype(WIDE)
        pass_o = pass_o.astype(WIDE) + part_o[k].astype(WIDE)
        if k:
            pass_p, pass_o = pass_p.astype(LOW), pass_o.astype(LOW)
    grad_o = pass_o
    part_p = pass_p.astype(LOW).reshape(ny * nc * nl, rows, 3, channels).swapaxes(1, 2)
    got_feed, part_p = tied(got_feed, part_p)
    got_feed = exchanged(got_feed.reshape(nh * nc, rows, -1), FEED)
    *done, sums_o = adam_columns(w_in, m_in, v_in, grad_o, 3 * D, 1)
    got_feed, part_p, sums_o = tied(got_feed, part_p, sums_o)
    got_p = exchanged(part_p, CONV)
    d_h_one = total(both, sent)
    d_values, d_gain_one = norm_backward(values, scale_one, gain_one, from_conv_order(d_h_one))
    input_grad = (d_values + d_middle).reshape(inputs.shape)

    tap_terms = jnp.stack(tap_grads, 1).reshape(1, 1, nh, 1, rows, TAPS)
    tap_terms = lax.dynamic_update_slice(
        jnp.zeros(sizes + (rows, TAPS), WIDE), tap_terms, (yi, ci, 0, li, 0, 0)
    )
    gain_terms = jnp.stack([d_gain_one, d_gain_two], 1).reshape(sizes + (rows, 2))
    terms = jnp.concatenate([tap_terms, gain_terms], -1).reshape(-1, rows, TAPS + 2)
    terms, got_feed = tied(terms, got_feed)
    *done, sums_wide = adam_gate(sizes, w_in, m_in, v_in, got_feed, done)
    got_p, terms, sums_wide = tied(got_p, terms, sums_wide)
    terms = exchanged(terms, AXES)
    *done, sums_p = adam_first(sizes, w_in, m_in, v_in, got_p, done)
    grad_down, sums_wide = tied(grad_down, sums_wide)
    grad_down, new_m_down, new_v_down, dir_down, sums_down = adam_down(w_down, m_down, v_down, grad_down)
    grad_in, new_m_in, new_v_in, dir_in = done
    block_out = (middle + out_sum.astype(WIDE)).astype(LOW).reshape(inputs.shape)
    terms = jnp.sum(terms, axis=0)
    grad_taps, grad_gains = terms[:, :TAPS], terms[:, TAPS:]
    new_m_taps, new_v_taps, dir_taps = adam_direction(conv_taps, grad_taps, m_taps, v_taps)
    new_m_gains, new_v_gains, dir_gains = adam_direction(norm_gains, grad_gains, m_gains, v_gains)

    def small(taps_like, gains_like):
        return jnp.concatenate(
            [jnp.sum(taps_like * taps_like)[None], jnp.sum(gains_like * gains_like, axis=0)]
        )

    sums = jnp.concatenate(
        [
            jnp.sum(jnp.concatenate([sums_p, sums_o, sums_wide, sums_down], 0), axis=(2, 3)),
            jnp.stack([small(conv_taps, norm_gains), small(dir_taps, dir_gains)], 1),
        ],
        0,
    )
    lamb_norms = jnp.sqrt(jnp.sum(spread_to(sums, AXES), axis=0).T)
    ratio = -RATE * lamb_norms[0] / (lamb_norms[1] + 1e-06)
    new_w_in = stepped(ratio[:4], w_in, dir_in)
    new_w_down = w_down + dir_down * ratio[4]
    new_w_taps = conv_taps + dir_taps * ratio[5]
    new_w_gains = norm_gains + dir_gains * ratio[6:][None, :]
    return (
        block_out,
        input_grad,
        grad_in,
        grad_down,
        grad_taps,
        grad_gains,
        new_m_in,
        new_m_down,
        new_m_taps,
        new_m_gains,
        new_v_in,
        new_v_down,
        new_v_taps,
        new_v_gains,
        new_w_in,
        new_w_down,
        new_w_taps,
        new_w_gains,
        lamb_norms,
    )


def solution(mesh):
    seq, shard = mesh.shape["seq"], mesh.shape["shard"]
    grid = Mesh(mesh.devices.reshape(seq // 2, 2, 4, shard // 4), AXES)
    tokens = P(("h", "l"), ("y", "c"), None)
    weights = P(AXES, None)
    return jax.shard_map(
        local,
        mesh=grid,
        in_specs=(tokens, tokens, P(("h", "l"), ("y", "c"))) + (weights,) * 12,
        out_specs=(tokens, tokens) + (weights,) * 16 + (P(),),
        check_vma=False,
    )
```

```python
import functools

import jax
import jax.numpy as jnp
import numpy as np
from jax import lax
from jax.experimental import pallas as pl
from jax.experimental.pallas import tpu as pltpu
from jax.sharding import Mesh
from jax.sharding import PartitionSpec as P

D = 2048
FF = 8192
TAPS = 3
STEP = 4


EPS_NORM = 1e-05
BETA_ONE = 0.9
BETA_TWO = 0.999
EPS_ADAM = 1e-08
DECAY = 0.01
RATE = 0.3

AXES = ("y", "c", "h", "l")
FEED = ("h", "c")
FEED_COPIES = ("y", "l")
CONV = ("y", "c", "l")
LINES = ("l", "y")
LOW = jnp.bfloat16
WIDE = jnp.float32
ROOM = 56 * 1024 * 1024
SHORT = pl.CostEstimate(flops=1024, bytes_accessed=1024, transcendentals=0)


def turned(value, axes, steps):
    n = lax.axis_size(axes)
    names = (axes,) if isinstance(axes, str) else axes
    ordered = tuple(a for a in AXES if a in names)
    where = np.arange(n).reshape([lax.axis_size(a) for a in ordered])
    where = where.transpose([ordered.index(a) for a in names]).reshape(-1)
    pairs = [(int(where[i]), int(where[(i + steps) % n])) for i in range(n)]
    return lax.ppermute(value, ordered if len(names) > 1 else axes, pairs)


def tied(*values):
    return lax.optimization_barrier(values)


def picked(value, index, dim):
    return lax.dynamic_index_in_dim(value, index, dim, keepdims=False)


def exchanged(value, axes):
    return lax.all_to_all(value, axes, 0, 0, tiled=True)


def spread_to(value, axes):
    return exchanged(jnp.broadcast_to(value[None], (lax.axis_size(axes),) + value.shape), axes)


def rolled(value, axis, dim, sign):
    n, me = lax.axis_size(axis), lax.axis_index(axis)
    twice = jnp.concatenate([value, value], dim)
    return lax.dynamic_slice_in_dim(twice, (sign * me) % n, n, dim)


def placed(pieces, axis):
    n, me = len(pieces), lax.axis_index(axis)
    out = jnp.zeros((n,) + pieces[0].shape, pieces[0].dtype)
    for k, piece in enumerate(pieces):
        out = lax.dynamic_update_slice(
            out, piece[None], ((me + k) % n,) + (0,) * piece.ndim
        )
    return out


def norm_forward(values, gain):
    scale = lax.rsqrt(jnp.mean(values * values, axis=-1, keepdims=True) + EPS_NORM)
    return (values * scale * gain, scale)


def norm_backward(values, scale, gain, grad):
    along = grad * gain
    inner = jnp.mean(along * values, axis=-1, keepdims=True)
    d_values = scale * along - scale * scale * scale * values * inner
    d_gain = jnp.sum(grad * values * scale, axis=0)
    return (d_values, d_gain)


def times(left, right):
    return jnp.dot(left, right, preferred_element_type=WIDE)


def times_wide(left, right):
    return lax.dot_general(
        left, right, (((1,), (1,)), ((), ())), preferred_element_type=WIDE
    )


def over_tokens(left, right):
    return lax.dot_general(
        left, right, (((0,), (0,)), ((), ())), preferred_element_type=WIDE
    )


def adam_direction(weight, grad, first, second):
    new_first = BETA_ONE * first + (1.0 - BETA_ONE) * grad
    new_second = BETA_TWO * second + (1.0 - BETA_TWO) * grad * grad
    first_hat = new_first / (1.0 - BETA_ONE**STEP)
    second_hat = new_second / (1.0 - BETA_TWO**STEP)
    direction = first_hat / (jnp.sqrt(second_hat) + EPS_ADAM) + DECAY * weight
    return (new_first, new_second, direction)


def assembled_kernel(me_ref, *refs):
    out_ref, n = refs[-1], len(refs) - 1
    for k in range(n):
        out_ref[pl.ds((me_ref[0] + k) % n, 1)] = refs[k][...][None]


def assembled(me, pieces):
    rows, cols = pieces[0].shape
    n = len(pieces)
    out = pl.pallas_call(
        assembled_kernel,
        in_specs=[pl.BlockSpec(memory_space=pltpu.SMEM)]
        + [pl.BlockSpec(memory_space=pltpu.VMEM) for _ in pieces],
        out_specs=pl.BlockSpec(memory_space=pltpu.VMEM),
        out_shape=jax.ShapeDtypeStruct((n, rows, cols), LOW),
        compiler_params=pltpu.CompilerParams(vmem_limit_bytes=ROOM),
        cost_estimate=SHORT,
    )(me.reshape(1).astype(jnp.int32), *pieces)
    return out.reshape(n * rows, cols)


def interleaved_kernel(place_ref, mine_ref, other_ref, out_ref):
    out_ref[0, pl.ds(place_ref[1], 1)] = mine_ref[...][None]
    out_ref[0, pl.ds(1 - place_ref[1], 1)] = other_ref[...][None]


def interleaved(place, mine, other, own):
    n, cols = mine.shape[0] // own, mine.shape[1]
    block = pl.BlockSpec((own, cols), lambda i, p: (i, 0))
    return pl.pallas_call(
        interleaved_kernel,
        grid_spec=pltpu.PrefetchScalarGridSpec(
            num_scalar_prefetch=1,
            grid=(n,),
            in_specs=[block, block],
            out_specs=pl.BlockSpec((1, 2, own, cols), lambda i, p: ((p[0] + i) % n, 0, 0, 0)),
        ),
        out_shape=jax.ShapeDtypeStruct((n, 2, own, cols), mine.dtype),
        compiler_params=pltpu.CompilerParams(vmem_limit_bytes=ROOM),
        cost_estimate=SHORT,
    )(place.astype(jnp.int32), mine, other)


def feed_kernel(c_ref, h_ref, e_ref, g_ref, u_ref, d_ref, hid_ref, dg_ref, du_ref):
    step = 256
    grads = e_ref[...].reshape(h_ref.shape)
    for j in range(h_ref.shape[0] // step):
        at = slice(j * step, (j + 1) * step)
        gate = times(h_ref[at, :], g_ref[...])
        up = times(h_ref[at, :], u_ref[...])
        d_hidden = times_wide(grads[at, :], d_ref[...])
        sig = jax.nn.sigmoid(gate)
        activated = gate * sig
        hid_ref[at, :] = (activated * up).astype(LOW)
        dg_ref[at, :] = (d_hidden * up * (sig * (1.0 + gate * (1.0 - sig)))).astype(LOW)
        du_ref[at, :] = (d_hidden * activated).astype(LOW)


def feed(core, h, e, gate, up, down):
    count, features = h.shape[0], down.shape[0]
    tile = 256
    made = pl.BlockSpec((count, tile), lambda i, c: (0, i))
    return pl.pallas_call(
        feed_kernel,
        grid_spec=pltpu.PrefetchScalarGridSpec(
            num_scalar_prefetch=1,
            grid=(features // tile,),
            in_specs=[
                pl.BlockSpec((count, D), lambda i, c: (0, 0), pipeline_mode=pl.Buffered(1)),
                pl.BlockSpec(
                    (e.shape[0], 1) + e.shape[2:],
                    lambda i, c: (0, c[0], 0, 0),
                    pipeline_mode=pl.Buffered(1),
                ),
                pl.BlockSpec((D, tile), lambda i, c: (0, i)),
                pl.BlockSpec((D, tile), lambda i, c: (0, i)),
                pl.BlockSpec((tile, D), lambda i, c: (i, 0)),
            ],
            out_specs=[made] * 3,
        ),
        out_shape=[jax.ShapeDtypeStruct((count, features), LOW)] * 3,
        compiler_params=pltpu.CompilerParams(vmem_limit_bytes=ROOM),
        cost_estimate=SHORT,
    )(core, h, e, gate, up, down)


def down_kernel(c_ref, mine_ref, other_ref, mine_e_ref, other_e_ref, out_ref):
    rows = mine_ref.shape[0]
    total = over_tokens(mine_ref[...], mine_e_ref[...].reshape(rows, -1))
    total += over_tokens(other_ref[...], other_e_ref[...].reshape(rows, -1))
    out_ref[...] = total.astype(out_ref.dtype)


def down_grads(core, mine, other, e):
    count, features = mine.shape
    tile = 512
    side = (e.shape[0], 1) + e.shape[2:]
    return pl.pallas_call(
        down_kernel,
        grid_spec=pltpu.PrefetchScalarGridSpec(
            num_scalar_prefetch=1,
            grid=(features // tile,),
            in_specs=[
                pl.BlockSpec((count, tile), lambda i, c: (0, i)),
                pl.BlockSpec((count, tile), lambda i, c: (0, i)),
                pl.BlockSpec(side, lambda i, c: (0, c[0], 0, 0), pipeline_mode=pl.Buffered(1)),
                pl.BlockSpec(side, lambda i, c: (0, 1 - c[0], 0, 0), pipeline_mode=pl.Buffered(1)),
            ],
            out_specs=pl.BlockSpec((tile, D), lambda i, c: (i, 0)),
        ),
        out_shape=jax.ShapeDtypeStruct((features, D), LOW),
        compiler_params=pltpu.CompilerParams(vmem_limit_bytes=ROOM),
        cost_estimate=SHORT,
    )(core, mine, other, e, e)


def back_kernel(pairs, *refs):
    out_ref = refs[-1]
    total = None
    for left, right in zip(refs[:pairs], refs[pairs:-1]):
        part = times_wide(left[...], right[...])
        total = part if total is None else total + part
    out_ref[...] = total.astype(out_ref.dtype)


def back(lefts, right, dtype):
    count, width = lefts[0].shape
    tile = 512
    return pl.pallas_call(
        functools.partial(back_kernel, len(lefts)),
        grid=(D // tile,),
        in_specs=[
            pl.BlockSpec(a.shape, lambda i: (0, 0), pipeline_mode=pl.Buffered(1)) for a in lefts
        ]
        + [pl.BlockSpec((tile, width), lambda i, k=k: (i, k)) for k in range(len(lefts))],
        out_specs=pl.BlockSpec((count, tile), lambda i: (0, i)),
        out_shape=jax.ShapeDtypeStruct((count, D), dtype),
        compiler_params=pltpu.CompilerParams(vmem_limit_bytes=ROOM),
        cost_estimate=SHORT,
    )(*lefts, *[right] * len(lefts))


def both_kernel(count, wide, c_ref, *refs):
    out_ref = refs[-1]
    mine, other, rights = refs[:count], refs[count : 2 * count], refs[2 * count : -1]
    product = times_wide if wide else times

    def write(lefts):
        total = None
        for left, right in zip(lefts, rights):
            part = product(left[...], right[...])
            total = part if total is None else total + part
        out_ref[...] = total.astype(out_ref.dtype).reshape(out_ref.shape)

    @pl.when(pl.program_id(0) == 0)
    def _():
        write(mine)

    @pl.when(pl.program_id(0) == 1)
    def _():
        write(other)


def both_cores(core, mine, other, rights, own, wide):
    count, width = mine[0].shape
    tile = 512
    if wide:
        blocks = [pl.BlockSpec((tile, width), lambda g, i, c: (i, 0)) for _ in rights]
    else:
        blocks = [pl.BlockSpec((width, tile), lambda g, i, c: (0, i)) for _ in rights]
    return pl.pallas_call(
        functools.partial(both_kernel, len(mine), wide),
        grid_spec=pltpu.PrefetchScalarGridSpec(
            num_scalar_prefetch=1,
            grid=(2, D // tile),
            in_specs=[
                pl.BlockSpec(a.shape, lambda g, i, c: (0, 0), pipeline_mode=pl.Buffered(1))
                for a in mine + other
            ]
            + blocks,
            out_specs=pl.BlockSpec(
                (count // own, 1, own, tile), lambda g, i, c: (0, (c[0] + g) % 2, 0, i)
            ),
        ),
        out_shape=jax.ShapeDtypeStruct((count // own, 2, own, D), LOW),
        compiler_params=pltpu.CompilerParams(vmem_limit_bytes=ROOM),
        cost_estimate=SHORT,
    )(core, *mine, *other, *rights)


def weight_kernel(parts, outs, *refs):
    lefts, rights, out_ref = refs[:parts], refs[parts:-1], refs[-1]
    width = out_ref.shape[1] // outs
    for j in range(outs):
        total = None
        for i, left in enumerate(lefts):
            part = over_tokens(left[...], rights[i * outs + j][...])
            total = part if total is None else total + part
        out_ref[:, j * width : (j + 1) * width] = total.astype(out_ref.dtype)


def weight_grads(lefts, rights):
    parts, outs = len(lefts), len(rights[0])
    flat = [r for row in rights for r in row]
    rows, tile = lefts[0].shape[1], 512
    width = sum(r.shape[1] for r in rights[0])
    return pl.pallas_call(
        functools.partial(weight_kernel, parts, outs),
        grid=(rows // tile,),
        in_specs=[pl.BlockSpec((a.shape[0], tile), lambda i: (0, i)) for a in lefts]
        + [pl.BlockSpec(r.shape, lambda i: (0, 0), pipeline_mode=pl.Buffered(1)) for r in flat],
        out_specs=pl.BlockSpec((tile, width), lambda i: (i, 0)),
        out_shape=jax.ShapeDtypeStruct((rows, width), LOW),
        compiler_params=pltpu.CompilerParams(vmem_limit_bytes=ROOM),
        cost_estimate=SHORT,
    )(*lefts, *flat)


def prep_feed_kernel(nc, nh, w_ref, out_ref):
    width = out_ref.shape[2]
    for c in range(nc):
        for h in range(nh):
            at = (c * nh + h) * width
            out_ref[h * nc + c] = w_ref[:, at : at + width].astype(LOW)


def prep_feed(sizes, w, first):
    ny, nc, nh, _ = sizes
    rows, block = w.shape[0], FF // ny
    return pl.pallas_call(
        functools.partial(prep_feed_kernel, nc, nh),
        grid=(ny,),
        in_specs=[pl.BlockSpec((rows, block), lambda i: (0, first // block + i))],
        out_specs=pl.BlockSpec((nh * nc, rows, block // (nh * nc)), lambda i: (0, 0, i)),
        out_shape=jax.ShapeDtypeStruct((nh * nc, rows, FF // (nh * nc)), LOW),
        compiler_params=pltpu.CompilerParams(vmem_limit_bytes=ROOM),
        cost_estimate=SHORT,
    )(w)


def prep_conv_kernel(sizes, w_ref, out_ref):
    ny, nc, nh, nl = sizes
    rows = w_ref.shape[0]
    for yc in range(ny * nc):
        for k in range(nl):
            parts = [
                w_ref[:, ((yc * nh + h) * nl + k) * rows : ((yc * nh + h) * nl + k + 1) * rows]
                for h in range(nh)
            ]
            out_ref[yc * nl + k, 0] = jnp.concatenate(parts, 1).astype(LOW)


def prep_conv(sizes, w):
    ny, nc, nh, nl = sizes
    rows = w.shape[0]
    shape = (ny * nc * nl, 3, rows, nh * rows)
    return pl.pallas_call(
        functools.partial(prep_conv_kernel, sizes),
        grid=(3,),
        in_specs=[pl.BlockSpec((rows, D), lambda i: (0, i))],
        out_specs=pl.BlockSpec((shape[0], 1) + shape[2:], lambda i: (0, i, 0, 0)),
        out_shape=jax.ShapeDtypeStruct(shape, LOW),
        compiler_params=pltpu.CompilerParams(vmem_limit_bytes=ROOM),
        cost_estimate=SHORT,
    )(w)


def fold(values):
    rows, cols = values.shape
    total = values[:, :128]
    for k in range(1, cols // 128):
        total = total + values[:, 128 * k : 128 * (k + 1)]
    out = total[:8]
    for k in range(1, rows // 8):
        out = out + total[8 * k : 8 * (k + 1)]
    return out


def adam_step(first, grad, w_ref, m_ref, v_ref, grad_ref, nm_ref, nv_ref, dir_ref, sum_ref):
    weight = w_ref[...]
    new_m, new_v, direction = adam_direction(weight, grad, m_ref[...], v_ref[...])
    grad_ref[...] = grad
    nm_ref[...] = new_m
    nv_ref[...] = new_v
    dir_ref[...] = direction

    @pl.when(first)
    def _():
        sum_ref[...] = jnp.zeros_like(sum_ref)

    sum_ref[0, 0] += fold(weight * weight)
    sum_ref[0, 1] += fold(direction * direction)


def adam_gate_kernel(w_ref, m_ref, v_ref, got_ref, *refs):
    grad = jnp.concatenate([got_ref[h, 0] for h in range(got_ref.shape[0])], 1).astype(WIDE)
    adam_step(pl.program_id(1) == 0, grad, w_ref, m_ref, v_ref, *refs[-5:])


def adam_gate(sizes, w, m, v, got, done=()):
    ny, nc, nh, _ = sizes
    rows = w.shape[0]
    part = got.shape[2] // (2 * ny)
    width = nh * part
    blocks = ny * nc
    column = pl.BlockSpec((rows, width), lambda k, b: (0, 4 * D // width + k * blocks + b))
    like = jax.ShapeDtypeStruct(w.shape, WIDE)
    return pl.pallas_call(
        adam_gate_kernel,
        grid=(2, blocks),
        in_specs=[column] * 3
        + [pl.BlockSpec((nh, 1, rows, part), lambda k, b: (0, b % nc, 0, k * ny + b // nc))]
        + [pl.BlockSpec(memory_space=pl.ANY) for _ in done],
        out_specs=[column] * 4 + [pl.BlockSpec((1, 2, 8, 128), lambda k, b: (k, 0, 0, 0))],
        out_shape=[like] * 4 + [jax.ShapeDtypeStruct((2, 2, 8, 128), WIDE)],
        input_output_aliases={4 + k: k for k in range(len(done))},
        compiler_params=pltpu.CompilerParams(vmem_limit_bytes=ROOM),
        cost_estimate=SHORT,
    )(w, m, v, got.reshape(nh, nc, rows, -1), *done)


def adam_plain_kernel(w_ref, m_ref, v_ref, g_ref, *refs):
    adam_step(pl.program_id(1) == 0, g_ref[...].astype(WIDE), w_ref, m_ref, v_ref, *refs[-5:])


def adam_columns(w, m, v, grad, first, kinds, done=()):
    rows = w.shape[0]
    width = 1024
    blocks = grad.shape[1] // (kinds * width)
    column = pl.BlockSpec((rows, width), lambda k, b: (0, first // width + k * blocks + b))
    like = jax.ShapeDtypeStruct(w.shape, WIDE)
    return pl.pallas_call(
        adam_plain_kernel,
        grid=(kinds, blocks),
        in_specs=[column] * 3
        + [pl.BlockSpec((rows, width), lambda k, b: (0, k * blocks + b))]
        + [pl.BlockSpec(memory_space=pl.ANY) for _ in done],
        out_specs=[column] * 4 + [pl.BlockSpec((1, 2, 8, 128), lambda k, b: (k, 0, 0, 0))],
        out_shape=[like] * 4 + [jax.ShapeDtypeStruct((kinds, 2, 8, 128), WIDE)],
        input_output_aliases={4 + k: k for k in range(len(done))},
        compiler_params=pltpu.CompilerParams(vmem_limit_bytes=ROOM),
        cost_estimate=SHORT,
    )(w, m, v, grad, *done)


def adam_down(w, m, v, grad):
    rows = 64
    block = pl.BlockSpec((rows, D), lambda k, i: (i, 0))
    like = jax.ShapeDtypeStruct(w.shape, WIDE)
    return pl.pallas_call(
        adam_plain_kernel,
        grid=(1, w.shape[0] // rows),
        in_specs=[block] * 4,
        out_specs=[block] * 4 + [pl.BlockSpec((1, 2, 8, 128), lambda k, i: (0, 0, 0, 0))],
        out_shape=[like] * 4 + [jax.ShapeDtypeStruct((1, 2, 8, 128), WIDE)],
        compiler_params=pltpu.CompilerParams(vmem_limit_bytes=ROOM),
        cost_estimate=SHORT,
    )(w, m, v, grad)


def adam_first_kernel(sizes, w_ref, m_ref, v_ref, got_ref, *refs):
    ny, nc, nh, nl = sizes
    rows = w_ref.shape[0]
    parts = []
    for yc in range(ny * nc):
        for h in range(nh):
            for k in range(nl):
                parts.append(got_ref[yc * nl + k, 0, :, h * rows : (h + 1) * rows])
    grad = jnp.concatenate(parts, 1).astype(WIDE)
    adam_step(pl.program_id(0) == 0, grad, w_ref, m_ref, v_ref, *refs[-5:])


def adam_first(sizes, w, m, v, got, done=()):
    rows = w.shape[0]
    column = pl.BlockSpec((rows, D), lambda i: (0, i))
    like = jax.ShapeDtypeStruct(w.shape, WIDE)
    return pl.pallas_call(
        functools.partial(adam_first_kernel, sizes),
        grid=(3,),
        in_specs=[column] * 3
        + [pl.BlockSpec((got.shape[0], 1) + got.shape[2:], lambda i: (0, i, 0, 0))]
        + [pl.BlockSpec(memory_space=pl.ANY) for _ in done],
        out_specs=[column] * 4 + [pl.BlockSpec((1, 2, 8, 128), lambda i: (0, 0, 0, 0))],
        out_shape=[like] * 4 + [jax.ShapeDtypeStruct((1, 2, 8, 128), WIDE)],
        input_output_aliases={4 + k: k for k in range(len(done))},
        compiler_params=pltpu.CompilerParams(vmem_limit_bytes=ROOM),
        cost_estimate=SHORT,
    )(w, m, v, got, *done)


def step_kernel(count, ratio_ref, w_ref, dir_ref, out_ref):
    for k in range(count):
        block = pl.program_id(0) * count + k
        piece = jnp.where(block < 3, 0, jnp.where(block < 4, 1, jnp.where(block < 4 + FF // D, 2, 3)))
        at = slice(k * D, (k + 1) * D)
        out_ref[:, at] = w_ref[:, at] + dir_ref[:, at] * ratio_ref[piece]


def stepped(ratio, w, direction):
    rows, cols = w.shape
    count = 3
    column = pl.BlockSpec((rows, count * D), lambda b, r: (0, b))
    return pl.pallas_call(
        functools.partial(step_kernel, count),
        grid_spec=pltpu.PrefetchScalarGridSpec(
            num_scalar_prefetch=1,
            grid=(cols // (count * D),),
            in_specs=[column] * 2,
            out_specs=column,
        ),
        out_shape=jax.ShapeDtypeStruct(w.shape, WIDE),
        compiler_params=pltpu.CompilerParams(vmem_limit_bytes=ROOM),
        cost_estimate=SHORT,
    )(ratio, w, direction)


def local(
    inputs,
    out_grad,
    segments,
    w_in,
    w_down,
    conv_taps,
    norm_gains,
    m_in,
    m_down,
    m_taps,
    m_gains,
    v_in,
    v_down,
    v_taps,
    v_gains,
):
    sizes = tuple(lax.axis_size(a) for a in AXES)
    ny, nc, nh, nl = sizes
    yi, ci, hi, li = (lax.axis_index(a) for a in AXES)
    own = inputs.shape[0] * inputs.shape[1]
    rows = w_in.shape[0]
    wide_rows = w_down.shape[0]
    channels = nh * rows
    span = ny * nc * own
    conv_total = nl * span

    def feed_order(a):
        return a.reshape(own, ny, nc, nh, nl, rows).transpose(0, 1, 4, 3, 2, 5).reshape(own, D)

    def from_feed_order(a):
        return a.reshape(own, ny, nl, nh, nc, rows).transpose(0, 1, 4, 3, 2, 5).reshape(own, D)

    def conv_order(a):
        return rolled(a.reshape(own, ny * nc, nh, -1).swapaxes(1, 2), "h", 1, 1).reshape(own, D)

    def from_conv_order(a):
        return rolled(a.reshape(own, nh, ny * nc, -1), "h", 1, -1).swapaxes(1, 2).reshape(own, D)

    def near(value, axes, first=1, last=None):
        last = lax.axis_size(axes) if last is None else last
        return [turned(value, axes, -k) for k in range(first, last)]

    def ring(value, axis):
        pieces = [value]
        for _ in range(1, lax.axis_size(axis)):
            pieces.append(turned(pieces[-1], axis, -1))
        return pieces

    def ring_sum(blocks, axis):
        n = lax.axis_size(axis)
        passed = blocks[n - 1]
        for k in range(n - 2, -1, -1):
            passed = turned(passed.astype(LOW), axis, 1).astype(WIDE) + blocks[k].astype(WIDE)
        return passed

    def with_core(pieces):
        mine = jnp.concatenate(pieces, 0)
        return mine, turned(mine, "c", 1)

    def scatter(other, mine, axes):
        both = turned(other, "c", 1)
        both = (mine() + both.astype(WIDE)).reshape(-1, own, D)
        sent = [turned(both[k].astype(LOW), axes, k) for k in range(1, both.shape[0])]
        return both[0], sent

    def total(first, sent):
        for s in sent:
            first = first + s.astype(WIDE)
        return first

    def out_order(a):
        return rolled(a, "h", 0, -1)

    note = jnp.concatenate(
        [norm_gains.reshape(-1), conv_taps.reshape(-1), segments.reshape(-1).astype(WIDE)]
    )
    low_o = w_in[:, 3 * D : 4 * D].astype(LOW)
    notes, p_cols, low_o = tied(spread_to(note, AXES), prep_conv(sizes, w_in), low_o)
    o_pieces = [low_o] + near(low_o, "h")
    notes = notes.reshape(sizes + (-1,))
    gains = notes[..., : 2 * rows].reshape(D, 2).astype(LOW).astype(WIDE)
    gain_one = gains[:, 0]
    gain_two = gains[:, 1]
    of_group = picked(picked(picked(notes, li, 3), ci, 1), yi, 0)
    taps = of_group[:, 2 * rows : 5 * rows].reshape(channels, TAPS).astype(LOW).astype(WIDE)
    ids = picked(notes[..., 5 * rows :], hi, 2).transpose(2, 0, 1, 3).reshape(nl, span)

    def as_rows(a):
        return a.reshape(-1, a.shape[-1])

    grad_low = out_grad.reshape(own, D)
    grad_top = grad_low.astype(WIDE)
    down = lax.all_gather(w_down.astype(LOW), FEED_COPIES, axis=0, tiled=True)
    values = inputs.reshape(own, D).astype(WIDE)
    norm_one, scale_one = norm_forward(values, gain_one)
    low_one = conv_order(norm_one.astype(LOW))
    cols_p, low_one, *o_pieces = tied(exchanged(p_cols, CONV), low_one, *o_pieces)
    later, cols_p = tied(w_in, cols_p)
    gate_cols = prep_feed(sizes, later, 4 * D)
    h_pieces = [low_one] + near(low_one, LINES)
    gate_cols, up_cols, cols_p, down, h_pieces[1] = tied(
        exchanged(gate_cols, FEED), prep_feed(sizes, w_in, 4 * D + FF), cols_p, down, h_pieces[1]
    )
    mine, other = with_core(h_pieces)
    gate_w = lax.all_gather(as_rows(gate_cols), FEED_COPIES, axis=0, tiled=True)
    up_cols, cols_p = tied(exchanged(up_cols, FEED), cols_p)
    o_w = placed(o_pieces, "h").reshape(channels, D)
    pieces = [cols_p.swapaxes(1, 2).reshape(-1, 3 * channels)]
    for k in range(1, nh):
        piece = turned(pieces[-1], "h", -1)
        pieces.append(piece)
    pieces[-1], gate_w, grad_low = tied(pieces[-1], gate_w, grad_low)
    e_all = lax.all_gather(grad_low, FEED, axis=0)
    p_w = jnp.concatenate(pieces, 0)

    line = li * ny + yi
    h_one = interleaved(jnp.stack([line, ci]), mine, other, own).reshape(conv_total, D)
    bcx = times(h_one, p_w).reshape(nl, span, 3 * channels)
    b_part = bcx[:, :, :channels]
    c_part = bcx[:, :, channels : 2 * channels]
    x_part = bcx[:, :, 2 * channels :]
    mixed_in = b_part * x_part
    extended = jnp.pad(mixed_in, ((0, 0), (2, 0), (0, 0)))
    ext_ids = jnp.pad(ids, ((0, 0), (2, 0)), constant_values=-1.0)
    keeps = []
    conv = jnp.zeros((nl, span, channels), WIDE)
    for lag in range(TAPS):
        keep = (ext_ids[:, 2 - lag : 2 - lag + span] == ids).astype(WIDE)[:, :, None]
        keeps.append(keep)
        conv = conv + taps[:, lag] * extended[:, 2 - lag : 2 - lag + span] * keep
    y_mix = (c_part * conv).astype(LOW)

    def by_core(value):
        parts = rolled(value.reshape(ny * nl, nc, own, -1), LINES, 0, 1)
        return [picked(parts, (ci + k) % nc, 1).reshape(ny * nl * own, -1) for k in range(nc)]

    y_mine, y_other = by_core(y_mix)
    both, sent = scatter(times(y_other, o_w).astype(LOW), lambda: times(y_mine, o_w), LINES)
    up_cols, e_all, *sent = tied(up_cols, e_all, *sent)
    up_w = lax.all_gather(as_rows(up_cols), FEED_COPIES, axis=0, tiled=True)
    middle = values + total(both, sent)

    norm_two, scale_two = norm_forward(middle, gain_two)
    low_two = feed_order(norm_two.astype(LOW))
    h_mine = assembled(hi, [low_two] + near(low_two, "h"))
    h_other = turned(h_mine, "c", 1)
    e_all = e_all.reshape(nh, nc, own, D)
    core = ci.reshape(1).astype(jnp.int32)
    hid_mine, dg_mine, du_mine = feed(core, h_mine, e_all, gate_w, up_w, down)
    hid_other, dg_other, du_other = feed(1 - core, h_other, e_all, gate_w, up_w, down)
    def summed(part, axes):
        return lax.psum_scatter(part, axes, scatter_dimension=0, tiled=True)

    d_h_two = both_cores(core, [dg_mine, du_mine], [dg_other, du_other], [gate_w, up_w], own, True)
    d_h_two, h_mine = tied(d_h_two, h_mine)
    d_h_two = summed(d_h_two.reshape(-1, D), FEED).astype(WIDE)
    part_feed = weight_grads([h_mine, h_other], [[dg_mine, du_mine], [dg_other, du_other]])
    part_feed, hid_mine = tied(part_feed, hid_mine)
    part_down = down_grads(core, hid_mine, hid_other, e_all)
    out_part = both_cores(core, [hid_mine], [hid_other], [down], own, False)
    d_h_two, part_down, part_feed, out_part = tied(d_h_two, part_down, part_feed, out_part)
    out_sum = summed(out_part.reshape(-1, D), FEED)
    d_middle, d_gain_two = norm_backward(middle, scale_two, gain_two, from_feed_order(d_h_two))
    d_middle = d_middle + grad_top

    low_branch = d_middle.astype(LOW)
    do_mine, do_other = with_core([low_branch] + near(low_branch, LINES))
    do_mine, do_other, part_feed = tied(do_mine, do_other, part_feed)
    got_feed = summed(part_feed, FEED_COPIES)
    part_o = over_tokens(y_mine, do_mine) + over_tokens(y_other, do_other)
    part_o = rolled(part_o.reshape(nh, rows, D), "h", 0, 1)
    part_o = part_o.astype(LOW)
    d_mix = jnp.zeros((ny * nl, nc, own, channels), WIDE)
    for k, part in enumerate((do_mine, do_other)):
        part = rolled(times_wide(part, o_w).reshape(-1, 1, own, channels), LINES, 0, -1)
        d_mix = lax.dynamic_update_slice(d_mix, part, (0, (ci + k) % nc, 0, 0))
    d_mix = d_mix.reshape(nl, span, channels)
    d_c = d_mix * conv
    d_conv = d_mix * c_part
    d_extended = jnp.zeros((nl, span + 2, channels), WIDE)
    tap_grads = []
    for lag in range(TAPS):
        counted = d_conv * keeps[lag]
        tap_grads.append(jnp.sum(counted * extended[:, 2 - lag : 2 - lag + span], axis=(0, 1)))
        d_extended = d_extended + jnp.pad(taps[:, lag] * counted, ((0, 0), (2 - lag, lag), (0, 0)))
    d_mixed_in = d_extended[:, 2:]
    d_bcx = jnp.concatenate([d_mixed_in * x_part, d_c, d_mixed_in * b_part], 2).astype(LOW)

    part_p = weight_grads([h_one], [[d_bcx.reshape(conv_total, -1)]]).reshape(nh, -1, 3 * channels)
    part_p, part_o, d_bcx, part_down, out_sum = tied(part_p, part_o, d_bcx, part_down, out_sum)
    grad_down = summed(part_down, FEED_COPIES)
    db_mine, db_other = by_core(d_bcx)
    pass_p, pass_o = part_p[nh - 1], part_o[nh - 1]
    for k in range(nh - 2, -1, -1):
        pass_p, pass_o = turned(pass_p, "h", 1), turned(pass_o, "h", 1)
        if k == nh - 2:
            other = back([db_other], p_w, LOW)
            other, db_mine = tied(other, db_mine)
            both, sent = scatter(other, lambda: back([db_mine], p_w, WIDE), LINES)
            pass_p, pass_o, both = tied(pass_p, pass_o, both)
        if k == 0:
            pass_p, pass_o = tied(pass_p, pass_o)
        pass_p = pass_p.astype(WIDE) + part_p[k].astype(WIDE)
        pass_o = pass_o.astype(WIDE) + part_o[k].astype(WIDE)
        if k:
            pass_p, pass_o = pass_p.astype(LOW), pass_o.astype(LOW)
    grad_o = pass_o
    part_p = pass_p.astype(LOW).reshape(ny * nc * nl, rows, 3, channels).swapaxes(1, 2)
    got_feed, part_p = tied(got_feed, part_p)
    got_feed = exchanged(got_feed.reshape(nh * nc, rows, -1), FEED)
    *done, sums_o = adam_columns(w_in, m_in, v_in, grad_o, 3 * D, 1)
    got_feed, part_p, sums_o = tied(got_feed, part_p, sums_o)
    got_p = exchanged(part_p, CONV)
    d_h_one = total(both, sent)
    d_values, d_gain_one = norm_backward(values, scale_one, gain_one, from_conv_order(d_h_one))
    input_grad = (d_values + d_middle).reshape(inputs.shape)

    tap_terms = jnp.stack(tap_grads, 1).reshape(1, 1, nh, 1, rows, TAPS)
    tap_terms = lax.dynamic_update_slice(
        jnp.zeros(sizes + (rows, TAPS), WIDE), tap_terms, (yi, ci, 0, li, 0, 0)
    )
    gain_terms = jnp.stack([d_gain_one, d_gain_two], 1).reshape(sizes + (rows, 2))
    terms = jnp.concatenate([tap_terms, gain_terms], -1).reshape(-1, rows, TAPS + 2)
    terms, got_feed = tied(terms, got_feed)
    *done, sums_wide = adam_gate(sizes, w_in, m_in, v_in, got_feed, done)
    got_p, terms, sums_wide = tied(got_p, terms, sums_wide)
    terms = exchanged(terms, AXES)
    *done, sums_p = adam_first(sizes, w_in, m_in, v_in, got_p, done)
    grad_down, sums_wide = tied(grad_down, sums_wide)
    grad_down, new_m_down, new_v_down, dir_down, sums_down = adam_down(w_down, m_down, v_down, grad_down)
    grad_in, new_m_in, new_v_in, dir_in = done
    block_out = (middle + out_sum.astype(WIDE)).astype(LOW).reshape(inputs.shape)
    terms = jnp.sum(terms, axis=0)
    grad_taps, grad_gains = terms[:, :TAPS], terms[:, TAPS:]
    new_m_taps, new_v_taps, dir_taps = adam_direction(conv_taps, grad_taps, m_taps, v_taps)
    new_m_gains, new_v_gains, dir_gains = adam_direction(norm_gains, grad_gains, m_gains, v_gains)

    def small(taps_like, gains_like):
        return jnp.concatenate(
            [jnp.sum(taps_like * taps_like)[None], jnp.sum(gains_like * gains_like, axis=0)]
        )

    sums = jnp.concatenate(
        [
            jnp.sum(jnp.concatenate([sums_p, sums_o, sums_wide, sums_down], 0), axis=(2, 3)),
            jnp.stack([small(conv_taps, norm_gains), small(dir_taps, dir_gains)], 1),
        ],
        0,
    )
    lamb_norms = jnp.sqrt(jnp.sum(spread_to(sums, AXES), axis=0).T)
    ratio = -RATE * lamb_norms[0] / (lamb_norms[1] + 1e-06)
    new_w_in = stepped(ratio[:4], w_in, dir_in)
    new_w_down = w_down + dir_down * ratio[4]
    new_w_taps = conv_taps + dir_taps * ratio[5]
    new_w_gains = norm_gains + dir_gains * ratio[6:][None, :]
    return (
        block_out,
        input_grad,
        grad_in,
        grad_down,
        grad_taps,
        grad_gains,
        new_m_in,
        new_m_down,
        new_m_taps,
        new_m_gains,
        new_v_in,
        new_v_down,
        new_v_taps,
        new_v_gains,
        new_w_in,
        new_w_down,
        new_w_taps,
        new_w_gains,
        lamb_norms,
    )


def solution(mesh):
    seq, shard = mesh.shape["seq"], mesh.shape["shard"]
    grid = Mesh(mesh.devices.reshape(seq // 2, 2, 4, shard // 4), AXES)
    tokens = P(("h", "l"), ("y", "c"), None)
    weights = P(AXES, None)
    return jax.shard_map(
        local,
        mesh=grid,
        in_specs=(tokens, tokens, P(("h", "l"), ("y", "c"))) + (weights,) * 12,
        out_specs=(tokens, tokens) + (weights,) * 16 + (P(),),
        check_vma=False,
    )
```
